32 devices in a mesh: cont: 4 (over y, x), net: 8 (over z, core).
Axes of the slice: x: 2, y: 2, z: 4, core: 2. Of those that a mesh axis runs over, the one named last changes fastest.
Arguments:
- angles: float32 [256, 4096], P('cont', 'net'), may hold values from -6 to 6
- lam_from: float32 [256, 5120], P('cont', 'net'), may hold values from -4 to 4
- lam_to: float32 [256, 5120], P('cont', 'net'), may hold values from -4 to 4
- gen_dual: float32 [256, 4096], P('cont', 'net'), may hold values from -6 to 6
- base_prev: float32 [4096], P('net'), may hold values from 0 to 0.5
- outage: int32 [256, 5120], P('cont', 'net'), may hold values 0 or 1
- from_bus: int32 [5120], P('net'), may hold values from 0 to 511
- to_ref: int32 [5120], P('net'), may hold values from 0 to 639, as said below
- halo_rows: int32 [1024], P('net'), may hold values from 0 to 512, as said below
- stiffness: float32 [5120], P('net'), may hold values from 0.5 to 8
- bus_load: float32 [4096], P('net'), may hold values from -3 to 3
- gen_cost: float32 [4096], P('net'), may hold values from 0.25 to 4
- gen_limit: float32 [4096], P('net'), may hold values from 0.05 to 0.6
Outputs:
- angle_field: float32 [256, 4096], P('cont', 'net')
- generation: float32 [256, 4096], P('cont', 'net')
- base_setpoint: float32 [4096], P('net')
The draws below stay inside these ranges and needn't reach their ends.
Inputs may be any that keep to these rules, and one draw needn't show every extreme that they name: `halo_rows`: in each partition's 128 entries the live rows come first and are distinct buses of that partition, the rest equal 512; the first partition has no live entry; some partition has all 128 entries live, the others at least half. `to_ref`: A value below 512 is a bus of the branch's own partition; 512 + s names live slot s of the next partition's list; branches of the last partition are all local.
All inputs are finite; a program needn't handle non-finite values. No bound on the sum of `outage` on one device may be relied on, other than what follows from the above.
Results may differ from the reference program's by a relative error of at most 0.0001.
Values sent between devices are 32-bit elements; how exact they have to be, the bound alone decides.
No kernel may reach another device: no remote copies, remote signals or barrier semaphores. Data moves between devices by JAX's collectives and lax.ppermute only.
A program may use at most 64 MiB of HBM per device.

```python
import math
import jax
import jax.numpy as jnp

B_DEV = 512
HALO = 128
ROUNDS = 4
BR_DEV = 640
CONTS = 256
NB = 4096
NBR = 5120
N_NET = 8


def halo_layout(key):
    key_list = jax.random.split(jax.random.fold_in(key, 31), 6)
    index_net = jnp.arange(N_NET, dtype=jnp.int32)
    counts = jax.random.randint(key_list[0], (N_NET,), HALO // 2, HALO + 1)
    fullest = jax.random.randint(key_list[1], (), 1, N_NET)
    counts = jnp.where(index_net == fullest, HALO, counts)
    counts = jnp.where(index_net == 0, 0, counts)
    scores = jax.random.randint(key_list[2], (N_NET, B_DEV), 0, 1 << 18) * B_DEV + jnp.arange(B_DEV, dtype=jnp.int32)[None, :]
    ranked = jnp.argsort(scores, axis=1, stable=True)[:, :HALO].astype(jnp.int32)
    slot_ids = jnp.arange(HALO, dtype=jnp.int32)
    halo_list = jnp.where(slot_ids[None, :] < counts[:, None], ranked, B_DEV).reshape(-1)
    branch = jnp.arange(NBR, dtype=jnp.int32)
    owner = branch // BR_DEV
    remote = (jax.random.randint(key_list[3], (NBR,), 0, 8) < 3) & (owner < N_NET - 1)
    next_part = jnp.minimum(owner + 1, N_NET - 1)
    slot_index = jax.random.randint(key_list[4], (NBR,), 0, HALO) % jnp.maximum(counts[next_part], 1)
    local_bus = jax.random.randint(key_list[5], (NBR,), 0, B_DEV)
    targets = jnp.where(remote, B_DEV + slot_index, local_bus)
    return (halo_list.astype(jnp.int32), targets.astype(jnp.int32))


def draw_halo_rows(key, part):
    return halo_layout(key)[0]


def draw_to_ref(key, part):
    return halo_layout(key)[1]


def set_ends(drawn, rng, smallest, top_value):
    longest = drawn.shape.index(max(drawn.shape))
    spots = []
    for shift in (0, 1):
        where = [jax.random.randint(jax.random.fold_in(rng, axis), (), 0, length) for axis, length in enumerate(drawn.shape)]
        where[longest] = (where[longest] + shift) % drawn.shape[longest]
        spots.append(tuple(where))
    return drawn.at[spots[0]].set(smallest).at[spots[1]].set(top_value)


def shard_levels(rng, extent, shards, smallest, high):
    loudness = 1.0
    for dim, parts in shards:
        heights = jax.random.uniform(jax.random.fold_in(jax.random.fold_in(rng, 6), dim), (parts,), jnp.float32, smallest / len(shards), high / len(shards))
        loudness = loudness * jnp.repeat(jnp.exp(heights), extent[dim] // parts).reshape((-1,) + (1,) * (len(extent) - 1 - dim))
    return loudness


def normal_values(rng, extent, scale, limit, pieces=(), kind=jnp.bfloat16):
    result = scale * jax.random.normal(rng, extent, jnp.float32)
    if pieces:
        result = result * shard_levels(rng, extent, pieces, -0.22, 0.18)
    return jnp.clip(result, -limit, limit).astype(kind)


def setup_inputs(seed: int = 0) -> dict:
    keys = jax.random.split(jax.random.key(seed), 14)
    angles = normal_values(keys[0], (CONTS, NB), 1.0, 6.0, ((0, 4), (1, 8)), jnp.float32)
    lam_from = normal_values(keys[1], (CONTS, NBR), 0.5, 4.0, ((0, 4), (1, 8)), jnp.float32)
    lam_to = normal_values(keys[2], (CONTS, NBR), 0.5, 4.0, ((0, 4), (1, 8)), jnp.float32)
    gen_dual = normal_values(keys[3], (CONTS, NB), 1.0, 6.0, ((0, 4), (1, 8)), jnp.float32)
    base_prev = jnp.clip(0.5 * jax.random.uniform(keys[4], (NB,), jnp.float32) ** shard_levels(keys[4], (NB,), ((0, 8),), -0.2, 0.2), 0.0, 0.5)
    outage = set_ends((jax.random.randint(keys[5], (CONTS, NBR), 0, 8) < 1).astype(jnp.int32), jax.random.fold_in(keys[5], 1), 0, 1)
    from_bus = set_ends(jax.random.randint(keys[6], (NBR,), 0, B_DEV), jax.random.fold_in(keys[6], 1), 0, B_DEV - 1).astype(jnp.int32)
    to_ref = draw_to_ref(jax.random.fold_in(keys[13], 71), 0)
    halo_rows = draw_halo_rows(jax.random.fold_in(keys[13], 71), 0)
    stiffness = jnp.clip(jnp.exp(math.log(8.0) - 2.7725887 * jax.random.uniform(keys[9], (NBR,), jnp.float32) ** shard_levels(keys[9], (NBR,), ((0, 8),), -0.2, 0.2)), 0.5, 8.0)
    bus_load = normal_values(keys[10], (NB,), 0.5, 3.0, ((0, 8),), jnp.float32)
    gen_cost = jnp.clip(jnp.exp(math.log(4.0) - 2.7725887 * jax.random.uniform(keys[11], (NB,), jnp.float32) ** shard_levels(keys[11], (NB,), ((0, 8),), -0.2, 0.2)), 0.25, 4.0)
    gen_limit = jnp.clip(0.05 + 0.55 * jax.random.uniform(keys[12], (NB,), jnp.float32) ** shard_levels(keys[12], (NB,), ((0, 8),), -0.2, 0.2), 0.05, 0.6)
    return dict(angles=angles, lam_from=lam_from, lam_to=lam_to, gen_dual=gen_dual, base_prev=base_prev, outage=outage, from_bus=from_bus, to_ref=to_ref, halo_rows=halo_rows, stiffness=stiffness, bus_load=bus_load, gen_cost=gen_cost, gen_limit=gen_limit)


penalty = 1.0
balance = 2.0


def endpoints(from_bus, to_ref, halo_rows):
    owner = jnp.arange(NBR, dtype=jnp.int32) // BR_DEV
    from_global = owner * B_DEV + from_bus
    next_part = jnp.minimum(owner + 1, N_NET - 1)
    slot_index = jnp.clip(to_ref - B_DEV, 0, HALO - 1)
    remote_row = halo_rows[next_part * HALO + slot_index]
    to_global = jnp.where(to_ref < B_DEV, owner * B_DEV + to_ref, (owner + 1) * B_DEV + remote_row)
    to_global = jnp.clip(to_global, 0, NB - 1).astype(jnp.int32)
    return from_global.astype(jnp.int32), to_global


def reference(angles, lam_from, lam_to, gen_dual, base_prev, outage, from_bus, to_ref, halo_rows, stiffness, bus_load, gen_cost, gen_limit):
    from_global, to_global = endpoints(from_bus, to_ref, halo_rows)
    weighted = stiffness[None, :] * (1.0 - outage.astype(jnp.float32))
    degree = jnp.zeros((NB,), jnp.float32).at[from_global].add(1.0).at[to_global].add(1.0)
    theta = angles
    base_set = base_prev
    copy_from = jnp.zeros_like(lam_from)
    copy_to = jnp.zeros_like(lam_to)
    generation = jnp.zeros_like(gen_dual)
    for round_index in range(ROUNDS):
        if round_index > 0:
            lam_from = lam_from + penalty * (copy_from - theta[:, from_global])
            lam_to = lam_to + penalty * (copy_to - theta[:, to_global])
        target_from = theta[:, from_global] - lam_from / penalty
        target_to = theta[:, to_global] - lam_to / penalty
        angle_gap = penalty * (target_from - target_to) / (penalty + 2.0 * weighted)
        centre = 0.5 * (target_from + target_to)
        copy_from = centre + 0.5 * angle_gap
        copy_to = centre - 0.5 * angle_gap
        branch_flow = weighted * angle_gap
        zeros_field = jnp.zeros((CONTS, NB), jnp.float32)
        copy_sum = zeros_field.at[:, from_global].add(copy_from + lam_from / penalty).at[:, to_global].add(copy_to + lam_to / penalty)
        net_out = zeros_field.at[:, from_global].add(branch_flow).at[:, to_global].add(-branch_flow)
        theta = copy_sum / (degree + 1.0)[None, :]
        generation = (penalty * base_set[None, :] - gen_dual + balance * (bus_load[None, :] + net_out)) / (gen_cost + penalty + balance)[None, :]
        gen_dual = gen_dual + penalty * (generation - base_set[None, :])
        total = jnp.sum(generation + gen_dual / penalty, axis=0)
        base_set = jnp.clip(total / CONTS, 0.0, gen_limit)
    return theta, generation, base_set
```

```python
import jax
import jax.numpy as jnp
from jax import lax
from jax.experimental import pallas as pl
from jax.experimental.pallas import tpu as pltpu
from jax.sharding import PartitionSpec as P

ROUNDS = 4
PENALTY = 1.0
BALANCE = 2.0
F32 = jnp.float32
BF16 = jnp.bfloat16


def halves(value):
    high = value.astype(BF16)
    low = (value - high.astype(F32)).astype(BF16)
    return jnp.concatenate([high, low], axis=0)


def times(value, table):
    rows = value.shape[0]
    both = jnp.dot(halves(value), table, preferred_element_type=F32)
    return both[:rows] + both[rows:]


def times_t(value, table):
    rows = value.shape[0]
    both = lax.dot_general(
        halves(value), table, (((1,), (1,)), ((), ())), preferred_element_type=F32
    )
    return both[:rows] + both[rows:]


def column_ids(halo_row, buses):
    slots = halo_row.shape[1]
    own = jnp.where(halo_row < buses, halo_row, -1)
    away = buses + lax.broadcasted_iota(jnp.int32, (1, slots), 1)
    even = lax.axis_index("net") % 2 == 0
    first = jnp.where(even, away, own)
    second = jnp.where(even, own, away)
    return jnp.concatenate([first, second], axis=1)


def pick_kernel(theta_ref, halo_ref, pick1_ref, pick2_ref, own_ref):
    buses = theta_ref.shape[1]
    ids = column_ids(halo_ref[...], buses)
    rows = lax.broadcasted_iota(jnp.int32, (buses, ids.shape[1]), 0)
    table = jnp.where(rows == ids, 1.0, 0.0).astype(BF16)
    own_ref[...] = table
    pick = times(theta_ref[...], table)
    slots = halo_ref.shape[1]
    pick1_ref[...] = pick[:, :slots]
    pick2_ref[...] = pick[:, slots:]


def prep_kernel(
    theta_ref,
    lam_f_ref,
    lam_t_ref,
    outage_ref,
    from_ref,
    to_ref,
    halo_ref,
    stiff_ref,
    dual_ref,
    edge_ref,
    inner_ref,
    gain_ref,
    x_ref,
    p_ref,
    c_ref,
    count_edge_ref,
    count_inner_ref,
    sum_ref,
):
    buses = theta_ref.shape[1]
    branches = from_ref.shape[1]
    ids = column_ids(halo_ref[...], buses)
    edges = ids.shape[1]
    lanes = lax.broadcasted_iota(jnp.int32, (edges, buses), 1)
    ids_col = jnp.broadcast_to(ids, (edges, edges)).T[:, :1]
    inner = 1.0 - jnp.max(jnp.where(lanes == ids_col, 1.0, 0.0), axis=0, keepdims=True)
    bus_ids = lax.broadcasted_iota(jnp.int32, (1, buses), 1)
    inner_ids = jnp.where(inner > 0.0, bus_ids, -1)
    all_ids = jnp.concatenate([ids, inner_ids], axis=1)
    counts = jnp.zeros((8, all_ids.shape[1]), F32)
    step = 128
    for start in range(0, branches, step):
        part = slice(start, start + step)
        f_col = jnp.broadcast_to(from_ref[:, part], (step, step)).T[:, :1]
        t_col = jnp.broadcast_to(to_ref[:, part], (step, step)).T[:, :1]
        is_f = jnp.where(f_col == all_ids, 1.0, 0.0)
        is_t = jnp.where(t_col == all_ids, 1.0, 0.0)
        signed = (is_f - is_t).astype(BF16)
        edge_ref[part, :] = signed[:, :edges]
        inner_ref[part, :] = signed[:, edges:]
        ends = (is_f + is_t).reshape(step // 8, 8, all_ids.shape[1])
        counts = counts + jnp.sum(ends, axis=0)
    count = jnp.broadcast_to(jnp.sum(counts, axis=0, keepdims=True), counts.shape)
    count_edge_ref[...] = count[:, :edges]
    count_inner_ref[...] = count[:, edges:]
    weight = stiff_ref[...] * (1.0 - outage_ref[...].astype(F32))
    gain_ref[...] = PENALTY * weight / (PENALTY + 2.0 * weight)
    x = theta_ref[...] * inner
    x_ref[...] = x
    p = times_t(x, inner_ref[...])
    p_ref[...] = p
    c_ref[...] = p - (lam_f_ref[...] - lam_t_ref[...]) / PENALTY
    sum_ref[...] = jnp.broadcast_to(jnp.sum(dual_ref[...], axis=0, keepdims=True), sum_ref.shape)


def first_kernel(
    pick1_ref,
    pick2_ref,
    got1_ref,
    got2_ref,
    halo_ref,
    edge_ref,
    p_ref,
    c_ref,
    gain_ref,
    count_ref,
    send1_ref,
    send2_ref,
    z_ref,
    delta_ref,
    flow_ref,
):
    slots = halo_ref.shape[1]
    conts = p_ref.shape[0]
    even = lax.axis_index("net") % 2 == 0
    z1 = jnp.where(even, got1_ref[...], pick1_ref[...])
    z2 = jnp.where(even, pick2_ref[...], got2_ref[...])
    z = jnp.concatenate([z1, z2], axis=1)
    z_ref[...] = z
    moved = times_t(z, edge_ref[...])
    delta_ref[...] = p_ref[...] + moved
    flow = gain_ref[...] * (c_ref[...] + moved)
    flow_ref[...] = flow
    sums = times(flow, edge_ref[...])
    send1_ref[:conts, :] = sums[:, :slots]
    send2_ref[:conts, :] = sums[:, slots:]
    send1_ref[conts:, :] = count_ref[:, :slots]
    send2_ref[conts:, :] = count_ref[:, slots:]


def next_kernel(
    send1_ref,
    send2_ref,
    got1_ref,
    got2_ref,
    z_ref,
    degree_ref,
    edge_ref,
    p_ref,
    c_ref,
    gain_ref,
    out1_ref,
    out2_ref,
    z_out_ref,
    delta_ref,
    flow_ref,
    both_ref,
):
    conts = p_ref.shape[0]
    slots = out1_ref.shape[1]
    both = jnp.concatenate(
        [
            send1_ref[:conts, :] + got1_ref[:conts, :],
            send2_ref[:conts, :] + got2_ref[:conts, :],
        ],
        axis=1,
    )
    both_ref[...] = both
    degree = degree_ref[:1, :]
    z = (degree * z_ref[...] - both) / (degree + 1.0)
    z_out_ref[...] = z
    moved = times_t(z, edge_ref[...])
    delta_ref[...] = p_ref[...] + moved
    flow = gain_ref[...] * (c_ref[...] + 2.0 * moved)
    flow_ref[...] = flow
    sums = times(flow, edge_ref[...])
    out1_ref[...] = sums[:, :slots]
    out2_ref[...] = sums[:, slots:]


def second_kernel(
    send1_ref,
    send2_ref,
    got1_ref,
    got2_ref,
    z_ref,
    edge_ref,
    p_ref,
    c_ref,
    gain_ref,
    out1_ref,
    out2_ref,
    z_out_ref,
    delta_ref,
    flow_ref,
    both_ref,
    degree_ref,
):
    conts = p_ref.shape[0]
    degree_ref[...] = jnp.concatenate(
        [
            send1_ref[conts:, :] + got1_ref[conts:, :],
            send2_ref[conts:, :] + got2_ref[conts:, :],
        ],
        axis=1,
    )
    next_kernel(
        send1_ref,
        send2_ref,
        got1_ref,
        got2_ref,
        z_ref,
        degree_ref,
        edge_ref,
        p_ref,
        c_ref,
        gain_ref,
        out1_ref,
        out2_ref,
        z_out_ref,
        delta_ref,
        flow_ref,
        both_ref,
    )


def inner_step(flow_ref, x_ref, count_ref, inner_ref):
    net = times(flow_ref[...], inner_ref[...])
    count = count_ref[:1, :]
    return net, (count * x_ref[...] - net) / (count + 1.0)


def beside_kernel(
    flow_ref, delta_ref, x_ref, count_ref, inner_ref, net_ref, x_out_ref, p_ref, c_ref
):
    net, x = inner_step(flow_ref, x_ref, count_ref, inner_ref)
    net_ref[...] = net
    x_out_ref[...] = x
    p = times_t(x, inner_ref[...])
    p_ref[...] = p
    c_ref[...] = 2.0 * (p + flow_ref[...]) - delta_ref[...]


def beside_last_kernel(
    flow_ref,
    x_ref,
    count_ref,
    inner_ref,
    own_ref,
    dual_ref,
    cost_ref,
    dsum_ref,
    both0_ref,
    both1_ref,
    both2_ref,
    net0_ref,
    net1_ref,
    net2_ref,
    net_ref,
    x_out_ref,
    dual_out_ref,
    sums_ref,
):
    net, x = inner_step(flow_ref, x_ref, count_ref, inner_ref)
    net_ref[...] = net
    x_out_ref[...] = x
    conts = net.shape[0]
    edge = jnp.concatenate([both0_ref[...], both1_ref[...], both2_ref[...]], axis=0)
    spread = times_t(edge, own_ref[...])
    part = 1.0 / (cost_ref[...] + PENALTY + BALANCE)
    dual = dual_ref[...]
    sums_ref[0:1, :] = dsum_ref[:1, :]
    for index, ref in enumerate((net0_ref, net1_ref, net2_ref)):
        whole = ref[...] + spread[index * conts : (index + 1) * conts]
        sums_ref[index + 1 : index + 2, :] = jnp.sum(whole, axis=0, keepdims=True)
        dual = dual + part * (BALANCE * whole - dual)
    sums_ref[4:, :] = jnp.zeros((4, sums_ref.shape[1]), F32)
    dual_out_ref[...] = dual


def last_kernel(
    send1_ref,
    send2_ref,
    got1_ref,
    got2_ref,
    z_ref,
    degree_ref,
    own_ref,
    x_ref,
    net_ref,
    sums_in_ref,
    theta_ref,
    net_out_ref,
    sums_ref,
):
    conts = net_ref.shape[0]
    both = jnp.concatenate(
        [send1_ref[...] + got1_ref[...], send2_ref[...] + got2_ref[...]], axis=1
    )
    degree = degree_ref[:1, :]
    z = (degree * z_ref[...] - both) / (degree + 1.0)
    spread = times_t(jnp.concatenate([both, z], axis=0), own_ref[...])
    net = net_ref[...] + spread[:conts]
    net_out_ref[...] = net
    theta_ref[...] = x_ref[...] + spread[conts:]
    sums_ref[...] = sums_in_ref[...]
    sums_ref[4:5, :] = jnp.sum(net, axis=0, keepdims=True)


def end_kernel(
    contingencies,
    *refs,
):
    *sum_refs, base_ref, load_ref, cost_ref, limit_ref, dual_ref, net_ref, gen_ref, base_out_ref = refs
    total = sum_refs[0][...]
    for ref in sum_refs[1:]:
        total = total + ref[...]
    mean = total / contingencies
    base = base_ref[...]
    load = load_ref[...]
    limit = limit_ref[...]
    part = 1.0 / (cost_ref[...] + PENALTY + BALANCE)
    dual_mean = mean[0:1, :]
    shared = jnp.zeros_like(base)
    for index in range(ROUNDS):
        net_mean = mean[index + 1 : index + 2, :]
        if index == ROUNDS - 1:
            gen_ref[...] = part * (
                PENALTY * base - (dual_ref[...] + shared) + BALANCE * (load + net_ref[...])
            )
        gen_mean = part * (PENALTY * base - dual_mean + BALANCE * (load + net_mean))
        dual_mean = dual_mean + PENALTY * (gen_mean - base)
        shared = shared + PENALTY * (part * (PENALTY * base - shared + BALANCE * load) - base)
        base = jnp.clip(gen_mean + dual_mean / PENALTY, 0.0, limit)
    base_out_ref[...] = base


def call(kernel, outs, *args, flops=2 * 128 * 640 * 512):
    shapes = [jax.ShapeDtypeStruct(shape, dtype) for shape, dtype in outs]
    moved = sum(a.size * a.dtype.itemsize for a in args)
    return pl.pallas_call(
        kernel,
        out_shape=shapes,
        in_specs=[pl.BlockSpec(memory_space=pltpu.VMEM)] * len(args),
        out_specs=[pl.BlockSpec(memory_space=pltpu.VMEM)] * len(outs),
        compiler_params=pltpu.CompilerParams(vmem_limit_bytes=32 * 1024 * 1024),
        cost_estimate=pl.CostEstimate(flops=flops, bytes_accessed=moved, transcendentals=0),
    )(*args)


def swaps(conts, nets):
    def pairs(shift):
        found = []
        for c in range(conts):
            for p in range(nets):
                q = p + 1 if p % 2 == shift else p - 1
                if 0 <= q < nets:
                    found.append((c * nets + p, c * nets + q))
                elif (c ^ 1) < conts:
                    found.append((c * nets + p, (c ^ 1) * nets + p))
                else:
                    found.append((c * nets + p, c * nets + p))
        return found

    return pairs(0), pairs(1)


def local(
    angles,
    lam_from,
    lam_to,
    gen_dual,
    base_prev,
    outage,
    from_bus,
    to_ref,
    halo_rows,
    stiffness,
    bus_load,
    gen_cost,
    gen_limit,
):
    conts, buses = angles.shape
    branches = from_bus.shape[0]
    slots = halo_rows.shape[0]
    edges = 2 * slots
    cont_size = lax.axis_size("cont")
    net_size = lax.axis_size("net")
    swap1, swap2 = swaps(cont_size, net_size)
    axes = ("cont", "net")

    def trade(first, second):
        return lax.ppermute(first, axes, swap1), lax.ppermute(second, axes, swap2)

    from_row = from_bus.reshape(1, branches)
    to_row = to_ref.reshape(1, branches)
    halo_row = halo_rows.reshape(1, slots)
    stiff_row = stiffness.reshape(1, branches)
    base_row = base_prev.reshape(1, buses)
    load_row = bus_load.reshape(1, buses)
    cost_row = gen_cost.reshape(1, buses)
    limit_row = gen_limit.reshape(1, buses)

    bus = ((conts, buses), F32)
    branch = ((conts, branches), F32)
    half = ((conts, slots), F32)
    edge = ((conts, edges), F32)
    tall = ((conts + 8, slots), F32)

    pick1, pick2, own = call(
        pick_kernel, [half, half, ((buses, edges), BF16)], angles, halo_row
    )
    got1, got2 = trade(pick1, pick2)
    edge_table, inner_table, gain, x, p, c, count_edge, count_inner, dual_sum = call(
        prep_kernel,
        [
            ((branches, edges), BF16),
            ((branches, buses), BF16),
            branch,
            bus,
            branch,
            branch,
            ((8, edges), F32),
            ((8, buses), F32),
            ((8, buses), F32),
        ],
        angles,
        lam_from,
        lam_to,
        outage,
        from_row,
        to_row,
        halo_row,
        stiff_row,
        gen_dual,
    )
    send1, send2, z, delta, flow = call(
        first_kernel,
        [tall, tall, edge, branch, branch],
        pick1,
        pick2,
        got1,
        got2,
        halo_row,
        edge_table,
        p,
        c,
        gain,
        count_edge,
    )
    nets = []
    boths = []
    for index in range(1, ROUNDS):
        got1, got2 = trade(send1, send2)
        net, x, p, c = call(
            beside_kernel,
            [bus, bus, branch, branch],
            flow,
            delta,
            x,
            count_inner,
            inner_table,
        )
        nets.append(net)
        if index == 1:
            send1, send2, z, delta, flow, both, degree = call(
                second_kernel,
                [half, half, edge, branch, branch, edge, ((8, edges), F32)],
                send1,
                send2,
                got1,
                got2,
                z,
                edge_table,
                p,
                c,
                gain,
            )
        else:
            send1, send2, z, delta, flow, both = call(
                next_kernel,
                [half, half, edge, branch, branch, edge],
                send1,
                send2,
                got1,
                got2,
                z,
                degree,
                edge_table,
                p,
                c,
                gain,
            )
        boths.append(both)
    got1, got2 = trade(send1, send2)
    net, x, dual, sums = call(
        beside_last_kernel,
        [bus, bus, bus, ((8, buses), F32)],
        flow,
        x,
        count_inner,
        inner_table,
        own,
        gen_dual,
        cost_row,
        dual_sum,
        *boths,
        *nets,
    )
    theta, net, sums = call(
        last_kernel,
        [bus, bus, ((8, buses), F32)],
        send1,
        send2,
        got1,
        got2,
        z,
        degree,
        own,
        x,
        net,
        sums,
    )
    parts = [sums]
    for shift in range(1, cont_size):
        parts.append(
            lax.ppermute(sums, "cont", [(i, (i + shift) % cont_size) for i in range(cont_size)])
        )

    def finish(*refs):
        end_kernel(float(conts * cont_size), *refs)

    generation, base = call(
        finish,
        [bus, ((1, buses), F32)],
        *parts,
        base_row,
        load_row,
        cost_row,
        limit_row,
        dual,
        net,
    )
    return theta, generation, base.reshape(buses)


def solution(mesh):
    placed = (
        P("cont", "net"),
        P("cont", "net"),
        P("cont", "net"),
        P("cont", "net"),
        P("net"),
        P("cont", "net"),
        P("net"),
        P("net"),
        P("net"),
        P("net"),
        P("net"),
        P("net"),
        P("net"),
    )
    return jax.shard_map(
        local,
        mesh=mesh,
        in_specs=placed,
        out_specs=(P("cont", "net"), P("cont", "net"), P("net")),
        check_vma=False,
    )
```

```python
import jax
import jax.numpy as jnp
from jax import lax
from jax.experimental import pallas as pl
from jax.experimental.pallas import tpu as pltpu
from jax.sharding import PartitionSpec as P

ROUNDS = 4
PENALTY = 1.0
BALANCE = 2.0
F32 = jnp.float32
BF16 = jnp.bfloat16


def halves(value):
    high = value.astype(BF16)
    low = (value - high.astype(F32)).astype(BF16)
    return jnp.concatenate([high, low], axis=0)


def times(value, table):
    rows = value.shape[0]
    both = jnp.dot(halves(value), table, preferred_element_type=F32)
    return both[:rows] + both[rows:]


def times_t(value, table):
    rows = value.shape[0]
    both = lax.dot_general(
        halves(value), table, (((1,), (1,)), ((), ())), preferred_element_type=F32
    )
    return both[:rows] + both[rows:]


def column_ids(halo_row, buses):
    slots = halo_row.shape[1]
    own = jnp.where(halo_row < buses, halo_row, -1)
    away = buses + lax.broadcasted_iota(jnp.int32, (1, slots), 1)
    even = lax.axis_index("net") % 2 == 0
    first = jnp.where(even, away, own)
    second = jnp.where(even, own, away)
    return jnp.concatenate([first, second], axis=1)


def load_kernel(count, *refs):
    sources, targets = refs[:count], refs[count : 2 * count]
    pick1_ref, pick2_ref, own_ref, semaphores = refs[2 * count :]
    copies = [
        pltpu.make_async_copy(source, target, semaphores.at[index])
        for index, (source, target) in enumerate(zip(sources, targets))
    ]
    for copy in copies:
        copy.start()
    halo_ref, theta_ref = targets[:2]
    buses = theta_ref.shape[1]
    slots = halo_ref.shape[1]
    copies[0].wait()
    ids = column_ids(halo_ref[...], buses)
    rows = lax.broadcasted_iota(jnp.int32, (buses, ids.shape[1]), 0)
    table = jnp.where(rows == ids, 1.0, 0.0).astype(BF16)
    own_ref[...] = table
    copies[1].wait()
    pick = times(theta_ref[...], table)
    pick1_ref[...] = pick[:, :slots]
    pick2_ref[...] = pick[:, slots:]
    for copy in copies[2:]:
        copy.wait()


def prep_kernel(
    theta_ref,
    lam_f_ref,
    lam_t_ref,
    outage_ref,
    from_ref,
    to_ref,
    halo_ref,
    stiff_ref,
    dual_ref,
    base_ref,
    load_ref,
    cost_ref,
    limit_ref,
    edge_ref,
    inner_ref,
    gain_ref,
    x_ref,
    p_ref,
    c_ref,
    count_edge_ref,
    count_inner_ref,
    sum_ref,
    rows_ref,
):
    buses = theta_ref.shape[1]
    branches = from_ref.shape[1]
    ids = column_ids(halo_ref[...], buses)
    edges = ids.shape[1]
    lanes = lax.broadcasted_iota(jnp.int32, (edges, buses), 1)
    ids_col = jnp.broadcast_to(ids, (edges, edges)).T[:, :1]
    inner = 1.0 - jnp.max(jnp.where(lanes == ids_col, 1.0, 0.0), axis=0, keepdims=True)
    bus_ids = lax.broadcasted_iota(jnp.int32, (1, buses), 1)
    inner_ids = jnp.where(inner > 0.0, bus_ids, -1)
    all_ids = jnp.concatenate([ids, inner_ids], axis=1)
    counts = jnp.zeros((8, all_ids.shape[1]), F32)
    step = 128
    for start in range(0, branches, step):
        part = slice(start, start + step)
        f_col = jnp.broadcast_to(from_ref[:, part], (step, step)).T[:, :1]
        t_col = jnp.broadcast_to(to_ref[:, part], (step, step)).T[:, :1]
        is_f = jnp.where(f_col == all_ids, 1.0, 0.0)
        is_t = jnp.where(t_col == all_ids, 1.0, 0.0)
        signed = (is_f - is_t).astype(BF16)
        edge_ref[part, :] = signed[:, :edges]
        inner_ref[part, :] = signed[:, edges:]
        ends = (is_f + is_t).reshape(step // 8, 8, all_ids.shape[1])
        counts = counts + jnp.sum(ends, axis=0)
    count = jnp.broadcast_to(jnp.sum(counts, axis=0, keepdims=True), counts.shape)
    count_edge_ref[...] = count[:, :edges]
    count_inner_ref[...] = count[:, edges:]
    weight = stiff_ref[...] * (1.0 - outage_ref[...].astype(F32))
    gain_ref[...] = PENALTY * weight / (PENALTY + 2.0 * weight)
    x = theta_ref[...] * inner
    x_ref[...] = x
    p = times_t(x, inner_ref[...])
    p_ref[...] = p
    c_ref[...] = p - (lam_f_ref[...] - lam_t_ref[...]) / PENALTY
    sum_ref[...] = jnp.broadcast_to(jnp.sum(dual_ref[...], axis=0, keepdims=True), sum_ref.shape)
    for index, ref in enumerate((base_ref, load_ref, cost_ref, limit_ref)):
        rows_ref[2 * index : 2 * index + 2, :] = jnp.broadcast_to(ref[...], (2, buses))


def first_kernel(
    pick1_ref,
    pick2_ref,
    got1_ref,
    got2_ref,
    halo_ref,
    edge_ref,
    p_ref,
    c_ref,
    gain_ref,
    count_ref,
    send1_ref,
    send2_ref,
    z_ref,
    delta_ref,
    flow_ref,
):
    slots = halo_ref.shape[1]
    conts = p_ref.shape[0]
    even = lax.axis_index("net") % 2 == 0
    z1 = jnp.where(even, got1_ref[...], pick1_ref[...])
    z2 = jnp.where(even, pick2_ref[...], got2_ref[...])
    z = jnp.concatenate([z1, z2], axis=1)
    z_ref[...] = z
    moved = times_t(z, edge_ref[...])
    delta_ref[...] = p_ref[...] + moved
    flow = gain_ref[...] * (c_ref[...] + moved)
    flow_ref[...] = flow
    sums = times(flow, edge_ref[...])
    send1_ref[:conts, :] = sums[:, :slots]
    send2_ref[:conts, :] = sums[:, slots:]
    send1_ref[conts:, :] = count_ref[:, :slots]
    send2_ref[conts:, :] = count_ref[:, slots:]


def next_kernel(
    send1_ref,
    send2_ref,
    got1_ref,
    got2_ref,
    z_ref,
    degree_ref,
    edge_ref,
    p_ref,
    c_ref,
    gain_ref,
    out1_ref,
    out2_ref,
    z_out_ref,
    flow_ref,
    both_ref,
    delta_ref=None,
):
    conts = p_ref.shape[0]
    slots = out1_ref.shape[1]
    both = jnp.concatenate(
        [
            send1_ref[:conts, :] + got1_ref[:conts, :],
            send2_ref[:conts, :] + got2_ref[:conts, :],
        ],
        axis=1,
    )
    both_ref[...] = both
    degree = degree_ref[:1, :]
    z = (degree * z_ref[...] - both) / (degree + 1.0)
    z_out_ref[...] = z
    moved = times_t(z, edge_ref[...])
    if delta_ref is not None:
        delta_ref[...] = p_ref[...] + moved
    flow = gain_ref[...] * (c_ref[...] + 2.0 * moved)
    flow_ref[...] = flow
    sums = times(flow, edge_ref[...])
    out1_ref[...] = sums[:, :slots]
    out2_ref[...] = sums[:, slots:]


def second_kernel(
    send1_ref,
    send2_ref,
    got1_ref,
    got2_ref,
    z_ref,
    edge_ref,
    p_ref,
    c_ref,
    gain_ref,
    out1_ref,
    out2_ref,
    z_out_ref,
    flow_ref,
    both_ref,
    delta_ref,
    degree_ref,
):
    conts = p_ref.shape[0]
    degree_ref[...] = jnp.concatenate(
        [
            send1_ref[conts:, :] + got1_ref[conts:, :],
            send2_ref[conts:, :] + got2_ref[conts:, :],
        ],
        axis=1,
    )
    next_kernel(
        send1_ref,
        send2_ref,
        got1_ref,
        got2_ref,
        z_ref,
        degree_ref,
        edge_ref,
        p_ref,
        c_ref,
        gain_ref,
        out1_ref,
        out2_ref,
        z_out_ref,
        flow_ref,
        both_ref,
        delta_ref,
    )


def inner_step(flow_ref, x_ref, count_ref, inner_ref):
    net = times(flow_ref[...], inner_ref[...])
    count = count_ref[:1, :]
    return net, (count * x_ref[...] - net) / (count + 1.0)


def beside_kernel(
    flow_ref, delta_ref, x_ref, count_ref, inner_ref, net_ref, x_out_ref, p_ref, c_ref
):
    net, x = inner_step(flow_ref, x_ref, count_ref, inner_ref)
    net_ref[...] = net
    x_out_ref[...] = x
    p = times_t(x, inner_ref[...])
    p_ref[...] = p
    c_ref[...] = 2.0 * (p + flow_ref[...]) - delta_ref[...]


def beside_last_kernel(
    flow_ref,
    x_ref,
    count_ref,
    inner_ref,
    own_ref,
    dual_ref,
    rows_ref,
    dsum_ref,
    both0_ref,
    both1_ref,
    both2_ref,
    net0_ref,
    net1_ref,
    net2_ref,
    net_ref,
    x_out_ref,
    dual_out_ref,
    sums_ref,
):
    net, x = inner_step(flow_ref, x_ref, count_ref, inner_ref)
    net_ref[...] = net
    x_out_ref[...] = x
    conts = net.shape[0]
    edge = jnp.concatenate([both0_ref[...], both1_ref[...], both2_ref[...]], axis=0)
    spread = times_t(edge, own_ref[...])
    part = 1.0 / (rows_ref[4:5, :] + PENALTY + BALANCE)
    dual = dual_ref[...]
    sums_ref[0:1, :] = dsum_ref[:1, :]
    for index, ref in enumerate((net0_ref, net1_ref, net2_ref)):
        whole = ref[...] + spread[index * conts : (index + 1) * conts]
        sums_ref[index + 1 : index + 2, :] = jnp.sum(whole, axis=0, keepdims=True)
        dual = dual + part * (BALANCE * whole - dual)
    tail = sums_ref.shape[0] - 4
    sums_ref[4:, :] = jnp.broadcast_to(jnp.sum(net, axis=0, keepdims=True), (tail, net.shape[1]))
    dual_out_ref[...] = dual


def total_kernel(send1_ref, send2_ref, got1_ref, got2_ref, own_ref, sums_in_ref, both_ref, sums_ref):
    both = jnp.concatenate(
        [send1_ref[...] + got1_ref[...], send2_ref[...] + got2_ref[...]], axis=1
    )
    both_ref[...] = both
    row = jnp.broadcast_to(jnp.sum(both, axis=0, keepdims=True), (8, both.shape[1]))
    sums_ref[...] = sums_in_ref[...]
    sums_ref[4:5, :] = sums_in_ref[4:5, :] + times_t(row, own_ref[...])[:1]


def field_kernel(
    both_ref,
    z_ref,
    degree_ref,
    own_ref,
    x_ref,
    net_ref,
    dual_ref,
    rows_ref,
    theta_ref,
    gen_ref,
):
    conts = net_ref.shape[0]
    both = both_ref[...]
    degree = degree_ref[:1, :]
    z = (degree * z_ref[...] - both) / (degree + 1.0)
    spread = times_t(jnp.concatenate([both, z], axis=0), own_ref[...])
    theta_ref[...] = x_ref[...] + spread[conts:]
    part = 1.0 / (rows_ref[4:5, :] + PENALTY + BALANCE)
    gen_ref[...] = part * (BALANCE * (net_ref[...] + spread[:conts]) - dual_ref[...])


def end_kernel(contingencies, *refs):
    *sum_refs, rows_ref, part_gen_ref, gen_ref, base_out_ref = refs
    total = sum_refs[0][...]
    for ref in sum_refs[1:]:
        total = total + ref[...]
    mean = total / contingencies
    base, load = rows_ref[0:1, :], rows_ref[2:3, :]
    limit = rows_ref[6:7, :]
    part = 1.0 / (rows_ref[4:5, :] + PENALTY + BALANCE)
    dual_mean = mean[0:1, :]
    shared = jnp.zeros_like(base)
    for index in range(ROUNDS):
        net_mean = mean[index + 1 : index + 2, :]
        gen_shared = part * (PENALTY * base - shared + BALANCE * load)
        if index == ROUNDS - 1:
            gen_ref[...] = part_gen_ref[...] + gen_shared
        gen_mean = part * (PENALTY * base - dual_mean + BALANCE * (load + net_mean))
        dual_mean = dual_mean + PENALTY * (gen_mean - base)
        shared = shared + PENALTY * (gen_shared - base)
        base = jnp.clip(gen_mean + dual_mean / PENALTY, 0.0, limit)
    base_out_ref[...] = base


def call(kernel, outs, *args, scratch=(), space=pltpu.VMEM, flops=2 * 128 * 640 * 512):
    shapes = [jax.ShapeDtypeStruct(shape, dtype) for shape, dtype in outs]
    moved = sum(a.size * a.dtype.itemsize for a in args)
    return pl.pallas_call(
        kernel,
        out_shape=shapes,
        in_specs=[pl.BlockSpec(memory_space=space)] * len(args),
        out_specs=[pl.BlockSpec(memory_space=pltpu.VMEM)] * len(outs),
        scratch_shapes=list(scratch),
        compiler_params=pltpu.CompilerParams(vmem_limit_bytes=32 * 1024 * 1024),
        cost_estimate=pl.CostEstimate(flops=flops, bytes_accessed=moved, transcendentals=0),
    )(*args)


def swaps(conts, nets):
    def pairs(shift):
        found = []
        for c in range(conts):
            for p in range(nets):
                q = p + 1 if p % 2 == shift else p - 1
                if 0 <= q < nets:
                    found.append((c * nets + p, c * nets + q))
                elif (c ^ 1) < conts:
                    found.append((c * nets + p, (c ^ 1) * nets + p))
                else:
                    found.append((c * nets + p, c * nets + p))
        return found

    return pairs(0), pairs(1)


def local(
    angles,
    lam_from,
    lam_to,
    gen_dual,
    base_prev,
    outage,
    from_bus,
    to_ref,
    halo_rows,
    stiffness,
    bus_load,
    gen_cost,
    gen_limit,
):
    conts, buses = angles.shape
    branches = from_bus.shape[0]
    slots = halo_rows.shape[0]
    edges = 2 * slots
    cont_size = lax.axis_size("cont")
    net_size = lax.axis_size("net")
    swap1, swap2 = swaps(cont_size, net_size)
    axes = ("cont", "net")

    def trade(first, second):
        far = lax.ppermute(second, axes, swap2)
        return lax.ppermute(first, axes, swap1), far

    halo_row = halo_rows.reshape(1, slots)
    base_row = base_prev.reshape(1, buses)
    load_row = bus_load.reshape(1, buses)
    cost_row = gen_cost.reshape(1, buses)
    limit_row = gen_limit.reshape(1, buses)

    bus = ((conts, buses), F32)
    branch = ((conts, branches), F32)
    half = ((conts, slots), F32)
    edge = ((conts, edges), F32)
    tall = ((conts + 8, slots), F32)

    fetched = [halo_row, angles, lam_from, lam_to, outage, gen_dual]
    fetched += [base_row, load_row, cost_row, limit_row, from_bus, to_ref, stiffness]

    def load(*refs):
        load_kernel(len(fetched), *refs)

    *here, pick1, pick2, own = call(
        load,
        [(a.shape, a.dtype) for a in fetched] + [half, half, ((buses, edges), BF16)],
        *[pltpu.with_memory_space_constraint(a, pltpu.HBM) for a in fetched],
        space=pltpu.HBM,
        scratch=[pltpu.SemaphoreType.DMA((len(fetched),))],
    )
    halo_row, angles, lam_from, lam_to, outage, gen_dual = here[:6]
    from_row, to_row, stiff_row = (a.reshape(1, branches) for a in here[10:])
    got1, got2 = trade(pick1, pick2)
    edge_table, inner_table, gain, x, p, c, count_edge, count_inner, dual_sum, rows = call(
        prep_kernel,
        [
            ((branches, edges), BF16),
            ((branches, buses), BF16),
            branch,
            bus,
            branch,
            branch,
            ((8, edges), F32),
            ((8, buses), F32),
            ((8, buses), F32),
            ((8, buses), F32),
        ],
        angles,
        lam_from,
        lam_to,
        outage,
        from_row,
        to_row,
        halo_row,
        stiff_row,
        gen_dual,
        *here[6:10],
    )
    send1, send2, z, delta, flow = call(
        first_kernel,
        [tall, tall, edge, branch, branch],
        pick1,
        pick2,
        got1,
        got2,
        halo_row,
        edge_table,
        p,
        c,
        gain,
        count_edge,
    )
    nets = []
    boths = []
    for index in range(1, ROUNDS):
        got1, got2 = trade(send1, send2)
        net, x, p, c = call(
            beside_kernel,
            [bus, bus, branch, branch],
            flow,
            delta,
            x,
            count_inner,
            inner_table,
        )
        nets.append(net)
        outs = [half, half, edge, branch, edge]
        if index == 1:
            send1, send2, z, flow, both, delta, degree = call(
                second_kernel,
                outs + [branch, ((8, edges), F32)],
                send1,
                send2,
                got1,
                got2,
                z,
                edge_table,
                p,
                c,
                gain,
            )
        else:
            if index < ROUNDS - 1:
                outs = outs + [branch]
            send1, send2, z, flow, both, *deltas = call(
                next_kernel,
                outs,
                send1,
                send2,
                got1,
                got2,
                z,
                degree,
                edge_table,
                p,
                c,
                gain,
            )
            delta = deltas[0] if deltas else None
        boths.append(both)
    got1, got2 = trade(send1, send2)
    net, x, dual, sums = call(
        beside_last_kernel,
        [bus, bus, bus, ((8, buses), F32)],
        flow,
        x,
        count_inner,
        inner_table,
        own,
        gen_dual,
        rows,
        dual_sum,
        *boths,
        *nets,
    )
    both, sums = call(
        total_kernel, [edge, ((8, buses), F32)], send1, send2, got1, got2, own, sums
    )
    parts = [sums]
    for shift in range(1, cont_size):
        parts.append(
            lax.ppermute(sums, "cont", [(i, (i + shift) % cont_size) for i in range(cont_size)])
        )

    theta, part_gen = call(
        field_kernel, [bus, bus], both, z, degree, own, x, net, dual, rows
    )

    def finish(*refs):
        end_kernel(float(conts * cont_size), *refs)

    generation, base = call(finish, [bus, ((1, buses), F32)], *parts, rows, part_gen)
    return theta, generation, base.reshape(buses)


def solution(mesh):
    placed = (
        P("cont", "net"),
        P("cont", "net"),
        P("cont", "net"),
        P("cont", "net"),
        P("net"),
        P("cont", "net"),
        P("net"),
        P("net"),
        P("net"),
        P("net"),
        P("net"),
        P("net"),
        P("net"),
    )
    return jax.shard_map(
        local,
        mesh=mesh,
        in_specs=placed,
        out_specs=(P("cont", "net"), P("cont", "net"), P("net")),
        check_vma=False,
    )
```

```python
import jax
import jax.numpy as jnp
from jax import lax
from jax.experimental import pallas as pl
from jax.experimental.pallas import tpu as pltpu
from jax.sharding import PartitionSpec as P

ROUNDS = 4
PENALTY = 1.0
BALANCE = 2.0
F32 = jnp.float32
BF16 = jnp.bfloat16


def halves(value):
    high = value.astype(BF16)
    low = (value - high.astype(F32)).astype(BF16)
    return jnp.concatenate([high, low], axis=0)


def times(value, table):
    rows = value.shape[0]
    both = jnp.dot(halves(value), table, preferred_element_type=F32)
    return both[:rows] + both[rows:]


def times_t(value, table):
    rows = value.shape[0]
    both = lax.dot_general(
        halves(value), table, (((1,), (1,)), ((), ())), preferred_element_type=F32
    )
    return both[:rows] + both[rows:]


def column_ids(halo_row, buses):
    slots = halo_row.shape[1]
    own = jnp.where(halo_row < buses, halo_row, -1)
    away = buses + lax.broadcasted_iota(jnp.int32, (1, slots), 1)
    even = lax.axis_index("net") % 2 == 0
    first = jnp.where(even, away, own)
    second = jnp.where(even, own, away)
    return jnp.concatenate([first, second], axis=1)


def fetch(sources, targets, semaphores):
    copies = [
        pltpu.make_async_copy(source, target, semaphores.at[index])
        for index, (source, target) in enumerate(zip(sources, targets))
    ]
    for copy in copies:
        copy.start()
    return copies


def load_kernel(count, *refs):
    sources, targets = refs[:count], refs[count : 2 * count]
    pick_ref, own_ref, semaphores = refs[2 * count :]
    copies = fetch(sources, targets, semaphores)
    halo_ref, theta_ref = targets[:2]
    buses = theta_ref.shape[1]
    slots = halo_ref.shape[1]
    copies[0].wait()
    ids = column_ids(halo_ref[...], buses)
    rows = lax.broadcasted_iota(jnp.int32, (buses, ids.shape[1]), 0)
    table = jnp.where(rows == ids, 1.0, 0.0).astype(BF16)
    own_ref[...] = table
    copies[1].wait()
    pick_ref[...] = times(theta_ref[...], table[:, slots:])
    for copy in copies[2:]:
        copy.wait()


def prep_kernel(
    lam_f_hbm,
    lam_t_hbm,
    outage_hbm,
    dual_hbm,
    base_hbm,
    load_hbm,
    cost_hbm,
    limit_hbm,
    theta_ref,
    from_ref,
    to_ref,
    halo_ref,
    stiff_ref,
    own_ref,
    dual_ref,
    pick_ref,
    edge_ref,
    inner_ref,
    gain_ref,
    x_ref,
    p_ref,
    c_ref,
    count_edge_ref,
    count_inner_ref,
    sum_ref,
    rows_ref,
    lam_f_ref,
    lam_t_ref,
    outage_ref,
    base_ref,
    load_ref,
    cost_ref,
    limit_ref,
    semaphores,
):
    sources = (
        lam_f_hbm, lam_t_hbm, outage_hbm, dual_hbm, base_hbm, load_hbm, cost_hbm, limit_hbm
    )
    targets = (
        lam_f_ref, lam_t_ref, outage_ref, dual_ref, base_ref, load_ref, cost_ref, limit_ref
    )
    copies = fetch(sources, targets, semaphores)
    buses = theta_ref.shape[1]
    branches = from_ref.shape[1]
    slots = halo_ref.shape[1]
    ids = column_ids(halo_ref[...], buses)
    edges = ids.shape[1]
    pick_ref[...] = times(theta_ref[...], own_ref[:, :slots])
    lanes = lax.broadcasted_iota(jnp.int32, (edges, buses), 1)
    ids_col = jnp.broadcast_to(ids, (edges, edges)).T[:, :1]
    inner = 1.0 - jnp.max(jnp.where(lanes == ids_col, 1.0, 0.0), axis=0, keepdims=True)
    bus_ids = lax.broadcasted_iota(jnp.int32, (1, buses), 1)
    inner_ids = jnp.where(inner > 0.0, bus_ids, -1)
    all_ids = jnp.concatenate([ids, inner_ids], axis=1)
    counts = jnp.zeros((8, all_ids.shape[1]), F32)
    step = 128
    for start in range(0, branches, step):
        part = slice(start, start + step)
        f_col = jnp.broadcast_to(from_ref[:, part], (step, step)).T[:, :1]
        t_col = jnp.broadcast_to(to_ref[:, part], (step, step)).T[:, :1]
        is_f = jnp.where(f_col == all_ids, 1.0, 0.0)
        is_t = jnp.where(t_col == all_ids, 1.0, 0.0)
        signed = (is_f - is_t).astype(BF16)
        edge_ref[part, :] = signed[:, :edges]
        inner_ref[part, :] = signed[:, edges:]
        ends = (is_f + is_t).reshape(step // 8, 8, all_ids.shape[1])
        counts = counts + jnp.sum(ends, axis=0)
    count = jnp.broadcast_to(jnp.sum(counts, axis=0, keepdims=True), counts.shape)
    count_edge_ref[...] = count[:, :edges]
    count_inner_ref[...] = count[:, edges:]
    x = theta_ref[...] * inner
    x_ref[...] = x
    p = times_t(x, inner_ref[...])
    p_ref[...] = p
    for copy in copies:
        copy.wait()
    weight = stiff_ref[...] * (1.0 - outage_ref[...].astype(F32))
    gain_ref[...] = PENALTY * weight / (PENALTY + 2.0 * weight)
    c_ref[...] = p - (lam_f_ref[...] - lam_t_ref[...]) / PENALTY
    sum_ref[...] = jnp.broadcast_to(jnp.sum(dual_ref[...], axis=0, keepdims=True), sum_ref.shape)
    for index, ref in enumerate((base_ref, load_ref, cost_ref, limit_ref)):
        rows_ref[2 * index : 2 * index + 2, :] = jnp.broadcast_to(ref[...], (2, buses))


def near_first_kernel(pick_ref, got_ref, edge_ref, p_ref, c_ref, z_ref, p_out_ref, c_out_ref):
    slots = pick_ref.shape[1]
    even = lax.axis_index("net") % 2 == 0
    z = jnp.where(even, got_ref[...], pick_ref[...])
    z_ref[...] = z
    moved = times_t(z, edge_ref[:, :slots])
    p_out_ref[...] = p_ref[...] + moved
    c_out_ref[...] = c_ref[...] + moved


def far_first_kernel(
    pick_ref,
    got_ref,
    edge_ref,
    p_ref,
    c_ref,
    gain_ref,
    count_ref,
    send_ref,
    z_ref,
    delta_ref,
    flow_ref,
):
    slots = pick_ref.shape[1]
    conts = p_ref.shape[0]
    table = edge_ref[:, slots:]
    even = lax.axis_index("net") % 2 == 0
    z = jnp.where(even, pick_ref[...], got_ref[...])
    z_ref[...] = z
    moved = times_t(z, table)
    delta_ref[...] = p_ref[...] + moved
    flow = gain_ref[...] * (c_ref[...] + moved)
    flow_ref[...] = flow
    send_ref[:conts, :] = times(flow, table)
    send_ref[conts:, :] = count_ref[:, slots:]


def traded(send_ref, got_ref, z_ref, both_ref, z_out_ref, degree):
    conts = z_ref.shape[0]
    both = send_ref[:conts, :] + got_ref[:conts, :]
    both_ref[...] = both
    z = (degree * z_ref[...] - both) / (degree + 1.0)
    z_out_ref[...] = z
    return z


def near(send_ref, got_ref, z_ref, degree, edge_ref, p_ref, c_ref, outs):
    both_ref, z_out_ref, p_out_ref, c_out_ref = outs
    slots = z_ref.shape[1]
    z = traded(send_ref, got_ref, z_ref, both_ref, z_out_ref, degree)
    moved = times_t(z, edge_ref[:, :slots])
    p_out_ref[...] = p_ref[...] + moved
    c_out_ref[...] = c_ref[...] + 2.0 * moved


def near_second_kernel(send_ref, got_ref, z_ref, edge_ref, p_ref, c_ref, *outs):
    conts = z_ref.shape[0]
    *outs, degree_ref = outs
    degree = send_ref[conts:, :] + got_ref[conts:, :]
    degree_ref[...] = degree
    near(send_ref, got_ref, z_ref, degree[:1, :], edge_ref, p_ref, c_ref, outs)


def near_kernel(send_ref, got_ref, z_ref, degree_ref, edge_ref, p_ref, c_ref, *outs):
    near(send_ref, got_ref, z_ref, degree_ref[:1, :], edge_ref, p_ref, c_ref, outs)


def far(send_ref, got_ref, z_ref, degree, edge_ref, p_ref, c_ref, gain_ref, outs):
    both_ref, z_out_ref, flow_ref, out_ref, *deltas = outs
    slots = z_ref.shape[1]
    table = edge_ref[:, slots:]
    z = traded(send_ref, got_ref, z_ref, both_ref, z_out_ref, degree)
    moved = times_t(z, table)
    for delta_ref in deltas:
        delta_ref[...] = p_ref[...] + moved
    flow = gain_ref[...] * (c_ref[...] + 2.0 * moved)
    flow_ref[...] = flow
    out_ref[...] = times(flow, table)


def far_second_kernel(send_ref, got_ref, z_ref, edge_ref, p_ref, c_ref, gain_ref, *outs):
    conts = z_ref.shape[0]
    *outs, degree_ref = outs
    degree = send_ref[conts:, :] + got_ref[conts:, :]
    degree_ref[...] = degree
    far(send_ref, got_ref, z_ref, degree[:1, :], edge_ref, p_ref, c_ref, gain_ref, outs)


def far_kernel(send_ref, got_ref, z_ref, degree_ref, edge_ref, p_ref, c_ref, gain_ref, *outs):
    far(send_ref, got_ref, z_ref, degree_ref[:1, :], edge_ref, p_ref, c_ref, gain_ref, outs)


def inner_step(flow_ref, x_ref, count_ref, inner_ref, edge_ref, send_ref):
    flow = flow_ref[...]
    conts = flow.shape[0]
    slots = send_ref.shape[1]
    send_ref[:conts, :] = times(flow, edge_ref[:, :slots])
    net = times(flow, inner_ref[...])
    count = count_ref[:1, :]
    return net, (count * x_ref[...] - net) / (count + 1.0)


def beside_kernel(
    flow_ref,
    delta_ref,
    x_ref,
    count_ref,
    inner_ref,
    edge_ref,
    *refs,
):
    *counts, net_ref, x_out_ref, p_ref, c_ref, send_ref = refs
    conts, slots = flow_ref.shape[0], send_ref.shape[1]
    for ref in counts:
        send_ref[conts:, :] = ref[:, :slots]
    net, x = inner_step(flow_ref, x_ref, count_ref, inner_ref, edge_ref, send_ref)
    net_ref[...] = net
    x_out_ref[...] = x
    p = times_t(x, inner_ref[...])
    p_ref[...] = p
    c_ref[...] = 2.0 * (p + flow_ref[...]) - delta_ref[...]


def send_last_kernel(flow_ref, edge_ref, send_ref):
    send_ref[...] = times(flow_ref[...], edge_ref[:, : send_ref.shape[1]])


def beside_last_kernel(
    flow_ref,
    x_ref,
    count_ref,
    inner_ref,
    own_ref,
    dual_ref,
    rows_ref,
    dsum_ref,
    *refs,
):
    *refs, net_ref, x_out_ref, dual_out_ref, sums_ref = refs
    rounds = len(refs) // 3
    net = times(flow_ref[...], inner_ref[...])
    count = count_ref[:1, :]
    net_ref[...] = net
    x_out_ref[...] = (count * x_ref[...] - net) / (count + 1.0)
    conts = net.shape[0]
    edge = jnp.concatenate(
        [
            jnp.concatenate([refs[index][...], refs[rounds + index][...]], axis=1)
            for index in range(rounds)
        ],
        axis=0,
    )
    spread = times_t(edge, own_ref[...])
    part = 1.0 / (rows_ref[4:5, :] + PENALTY + BALANCE)
    dual = dual_ref[...]
    sums_ref[0:1, :] = dsum_ref[:1, :]
    for index, ref in enumerate(refs[2 * rounds :]):
        whole = ref[...] + spread[index * conts : (index + 1) * conts]
        sums_ref[index + 1 : index + 2, :] = jnp.sum(whole, axis=0, keepdims=True)
        dual = dual + part * (BALANCE * whole - dual)
    tail = sums_ref.shape[0] - rounds - 1
    sums_ref[rounds + 1 :, :] = jnp.broadcast_to(
        jnp.sum(net, axis=0, keepdims=True), (tail, net.shape[1])
    )
    dual_out_ref[...] = dual


def total_kernel(
    send1_ref, send2_ref, got1_ref, got2_ref, own_ref, sums_in_ref, both_ref, sums_ref
):
    both = jnp.concatenate(
        [send1_ref[...] + got1_ref[...], send2_ref[...] + got2_ref[...]], axis=1
    )
    both_ref[...] = both
    row = jnp.broadcast_to(jnp.sum(both, axis=0, keepdims=True), (8, both.shape[1]))
    sums_ref[...] = sums_in_ref[...]
    last = slice(ROUNDS, ROUNDS + 1)
    sums_ref[last, :] = sums_in_ref[last, :] + times_t(row, own_ref[...])[:1]


def field_kernel(
    both_ref,
    z1_ref,
    z2_ref,
    degree1_ref,
    degree2_ref,
    own_ref,
    x_ref,
    net_ref,
    dual_ref,
    rows_ref,
    theta_ref,
    gen_ref,
):
    conts = net_ref.shape[0]
    both = both_ref[...]
    old = jnp.concatenate([z1_ref[...], z2_ref[...]], axis=1)
    degree = jnp.concatenate([degree1_ref[:1, :], degree2_ref[:1, :]], axis=1)
    z = (degree * old - both) / (degree + 1.0)
    spread = times_t(jnp.concatenate([both, z], axis=0), own_ref[...])
    theta_ref[...] = x_ref[...] + spread[conts:]
    part = 1.0 / (rows_ref[4:5, :] + PENALTY + BALANCE)
    gen_ref[...] = part * (BALANCE * (net_ref[...] + spread[:conts]) - dual_ref[...])


def end_kernel(contingencies, *refs):
    *sum_refs, rows_ref, part_gen_ref, gen_ref, base_out_ref = refs
    total = sum_refs[0][...]
    for ref in sum_refs[1:]:
        total = total + ref[...]
    mean = total / contingencies
    base, load = rows_ref[0:1, :], rows_ref[2:3, :]
    limit = rows_ref[6:7, :]
    part = 1.0 / (rows_ref[4:5, :] + PENALTY + BALANCE)
    dual_mean = mean[0:1, :]
    shared = jnp.zeros_like(base)
    for index in range(ROUNDS):
        net_mean = mean[index + 1 : index + 2, :]
        gen_shared = part * (PENALTY * base - shared + BALANCE * load)
        if index == ROUNDS - 1:
            gen_ref[...] = part_gen_ref[...] + gen_shared
        gen_mean = part * (PENALTY * base - dual_mean + BALANCE * (load + net_mean))
        dual_mean = dual_mean + PENALTY * (gen_mean - base)
        shared = shared + PENALTY * (gen_shared - base)
        base = jnp.clip(gen_mean + dual_mean / PENALTY, 0.0, limit)
    base_out_ref[...] = base


def call(kernel, outs, *args, scratch=(), spaces=None, flops=2 * 128 * 640 * 512):
    shapes = [jax.ShapeDtypeStruct(shape, dtype) for shape, dtype in outs]
    moved = sum(a.size * a.dtype.itemsize for a in args)
    spaces = spaces or [pltpu.VMEM] * len(args)
    return pl.pallas_call(
        kernel,
        out_shape=shapes,
        in_specs=[pl.BlockSpec(memory_space=space) for space in spaces],
        out_specs=[pl.BlockSpec(memory_space=pltpu.VMEM)] * len(outs),
        scratch_shapes=list(scratch),
        compiler_params=pltpu.CompilerParams(vmem_limit_bytes=32 * 1024 * 1024),
        cost_estimate=pl.CostEstimate(flops=flops, bytes_accessed=moved, transcendentals=0),
    )(*args)


def swaps(conts, nets):
    def pairs(shift):
        found = []
        for c in range(conts):
            for p in range(nets):
                q = p + 1 if p % 2 == shift else p - 1
                if 0 <= q < nets:
                    found.append((c * nets + p, c * nets + q))
                elif (c ^ 1) < conts:
                    found.append((c * nets + p, (c ^ 1) * nets + p))
                else:
                    found.append((c * nets + p, c * nets + p))
        return found

    return pairs(0), pairs(1)


def local(
    angles,
    lam_from,
    lam_to,
    gen_dual,
    base_prev,
    outage,
    from_bus,
    to_ref,
    halo_rows,
    stiffness,
    bus_load,
    gen_cost,
    gen_limit,
):
    conts, buses = angles.shape
    branches = from_bus.shape[0]
    slots = halo_rows.shape[0]
    edges = 2 * slots
    cont_size = lax.axis_size("cont")
    net_size = lax.axis_size("net")
    swap1, swap2 = swaps(cont_size, net_size)
    axes = ("cont", "net")

    def trade_near(value):
        return lax.ppermute(value, axes, swap1)

    def trade_far(value):
        return lax.ppermute(value, axes, swap2)

    def in_hbm(*arrays):
        return [pltpu.with_memory_space_constraint(a, pltpu.HBM) for a in arrays]

    bus = ((conts, buses), F32)
    branch = ((conts, branches), F32)
    half = ((conts, slots), F32)
    edge = ((conts, edges), F32)
    tall = ((conts + 8, slots), F32)
    counts = ((8, slots), F32)
    row = ((8, buses), F32)

    halo_row = halo_rows.reshape(1, slots)
    fetched = [halo_row, angles, from_bus, to_ref, stiffness]
    number = len(fetched)

    def load(*refs):
        load_kernel(number, *refs)

    *here, pick2, own = call(
        load,
        [(a.shape, a.dtype) for a in fetched] + [half, ((buses, edges), BF16)],
        *in_hbm(*fetched),
        spaces=[pltpu.HBM] * number,
        scratch=[pltpu.SemaphoreType.DMA((number,))],
    )
    got2 = trade_far(pick2)
    halo_row, angles = here[:2]
    from_row, to_row, stiff_row = (a.reshape(1, branches) for a in here[2:])
    rows = [a.reshape(1, buses) for a in (base_prev, bus_load, gen_cost, gen_limit)]
    fetched = [lam_from, lam_to, outage, gen_dual, *rows]
    near_args = [angles, from_row, to_row, halo_row, stiff_row, own]
    (
        gen_dual,
        pick1,
        edge_table,
        inner_table,
        gain,
        x,
        p,
        c,
        count_edge,
        count_inner,
        dual_sum,
        rows,
    ) = call(
        prep_kernel,
        [
            bus,
            half,
            ((branches, edges), BF16),
            ((branches, buses), BF16),
            branch,
            bus,
            branch,
            branch,
            ((8, edges), F32),
            row,
            row,
            row,
        ],
        *in_hbm(*fetched),
        *near_args,
        spaces=[pltpu.HBM] * len(fetched) + [pltpu.VMEM] * len(near_args),
        scratch=[pltpu.VMEM(a.shape, a.dtype) for a in (lam_from, lam_to, outage)]
        + [pltpu.VMEM((1, buses), F32)] * 4
        + [pltpu.SemaphoreType.DMA((len(fetched),))],
    )
    got1 = trade_near(pick1)
    z1, p, c = call(near_first_kernel, [half, branch, branch], pick1, got1, edge_table, p, c)
    send2, z2, delta, flow = call(
        far_first_kernel,
        [tall, half, branch, branch],
        pick2,
        got2,
        edge_table,
        p,
        c,
        gain,
        count_edge,
    )
    nets, boths1, boths2 = [], [], []
    for index in range(1, ROUNDS):
        first = index == 1
        got2 = trade_far(send2)
        net, x, p, c, send1 = call(
            beside_kernel,
            [bus, bus, branch, branch, tall if first else half],
            flow,
            delta,
            x,
            count_inner,
            inner_table,
            edge_table,
            *([count_edge] if first else []),
        )
        nets.append(net)
        got1 = trade_near(send1)
        outs = [half, half, branch, branch]
        if first:
            both1, z1, p, c, degree1 = call(
                near_second_kernel, outs + [counts], send1, got1, z1, edge_table, p, c
            )
        else:
            both1, z1, p, c = call(
                near_kernel, outs, send1, got1, z1, degree1, edge_table, p, c
            )
        outs = [half, half, branch, half]
        if index < ROUNDS - 1:
            outs = outs + [branch]
        if first:
            both2, z2, flow, send2, *deltas, degree2 = call(
                far_second_kernel, outs + [counts], send2, got2, z2, edge_table, p, c, gain
            )
        else:
            both2, z2, flow, send2, *deltas = call(
                far_kernel, outs, send2, got2, z2, degree2, edge_table, p, c, gain
            )
        delta = deltas[0] if deltas else None
        boths1.append(both1)
        boths2.append(both2)
    got2 = trade_far(send2)
    (send1,) = call(send_last_kernel, [half], flow, edge_table)
    got1 = trade_near(send1)
    net, x, dual, sums = call(
        beside_last_kernel,
        [bus, bus, bus, row],
        flow,
        x,
        count_inner,
        inner_table,
        own,
        gen_dual,
        rows,
        dual_sum,
        *boths1,
        *boths2,
        *nets,
    )
    both, sums = call(total_kernel, [edge, row], send1, send2, got1, got2, own, sums)
    parts = [sums]
    for shift in range(1, cont_size):
        parts.append(
            lax.ppermute(sums, "cont", [(i, (i + shift) % cont_size) for i in range(cont_size)])
        )

    theta, part_gen = call(
        field_kernel,
        [bus, bus],
        both,
        z1,
        z2,
        degree1,
        degree2,
        own,
        x,
        net,
        dual,
        rows,
    )

    def finish(*refs):
        end_kernel(float(conts * cont_size), *refs)

    generation, base = call(finish, [bus, ((1, buses), F32)], *parts, rows, part_gen)
    return theta, generation, base.reshape(buses)


def solution(mesh):
    placed = (
        P("cont", "net"),
        P("cont", "net"),
        P("cont", "net"),
        P("cont", "net"),
        P("net"),
        P("cont", "net"),
        P("net"),
        P("net"),
        P("net"),
        P("net"),
        P("net"),
        P("net"),
        P("net"),
    )
    return jax.shard_map(
        local,
        mesh=mesh,
        in_specs=placed,
        out_specs=(P("cont", "net"), P("cont", "net"), P("net")),
        check_vma=False,
    )
```

```python
import jax
import jax.numpy as jnp
from jax import lax
from jax.experimental import pallas as pl
from jax.experimental.pallas import tpu as pltpu
from jax.sharding import PartitionSpec as P

ROUNDS = 4
PENALTY = 1.0
BALANCE = 2.0
F32 = jnp.float32
BF16 = jnp.bfloat16


def halves(value):
    high = value.astype(BF16)
    low = (value - high.astype(F32)).astype(BF16)
    return jnp.concatenate([high, low], axis=0)


def times(value, table):
    rows = value.shape[0]
    both = jnp.dot(halves(value), table, preferred_element_type=F32)
    return both[:rows] + both[rows:]


def times_t(value, table):
    rows = value.shape[0]
    both = lax.dot_general(
        halves(value), table, (((1,), (1,)), ((), ())), preferred_element_type=F32
    )
    return both[:rows] + both[rows:]


def column_ids(halo_row, buses):
    slots = halo_row.shape[1]
    own = jnp.where(halo_row < buses, halo_row, -1)
    away = buses + lax.broadcasted_iota(jnp.int32, (1, slots), 1)
    even = lax.axis_index("net") % 2 == 0
    first = jnp.where(even, away, own)
    second = jnp.where(even, own, away)
    return jnp.concatenate([first, second], axis=1)


def fetch(sources, targets, semaphores):
    copies = [
        pltpu.make_async_copy(source, target, semaphores.at[index])
        for index, (source, target) in enumerate(zip(sources, targets))
    ]
    for copy in copies:
        copy.start()
    return copies


def load_kernel(count, *refs):
    sources, targets = refs[:count], refs[count : 2 * count]
    pick_ref, own_ref, semaphores = refs[2 * count :]
    copies = fetch(sources, targets, semaphores)
    halo_ref, theta_ref = targets[:2]
    buses = theta_ref.shape[1]
    slots = halo_ref.shape[1]
    copies[0].wait()
    ids = column_ids(halo_ref[...], buses)
    rows = lax.broadcasted_iota(jnp.int32, (buses, ids.shape[1]), 0)
    table = jnp.where(rows == ids, 1.0, 0.0).astype(BF16)
    own_ref[...] = table
    copies[1].wait()
    pick_ref[...] = times(theta_ref[...], table[:, slots:])
    for copy in copies[2:]:
        copy.wait()


def prep_kernel(
    lam_f_hbm,
    lam_t_hbm,
    outage_hbm,
    dual_hbm,
    base_hbm,
    load_hbm,
    cost_hbm,
    limit_hbm,
    theta_ref,
    from_ref,
    to_ref,
    halo_ref,
    stiff_ref,
    own_ref,
    dual_ref,
    pick_ref,
    edge_ref,
    inner_ref,
    gain_ref,
    x_ref,
    p_ref,
    c_ref,
    count_edge_ref,
    count_inner_ref,
    sum_ref,
    rows_ref,
    lam_f_ref,
    lam_t_ref,
    outage_ref,
    base_ref,
    load_ref,
    cost_ref,
    limit_ref,
    semaphores,
):
    sources = (
        lam_f_hbm, lam_t_hbm, outage_hbm, dual_hbm, base_hbm, load_hbm, cost_hbm, limit_hbm
    )
    targets = (
        lam_f_ref, lam_t_ref, outage_ref, dual_ref, base_ref, load_ref, cost_ref, limit_ref
    )
    copies = fetch(sources, targets, semaphores)
    buses = theta_ref.shape[1]
    branches = from_ref.shape[1]
    slots = halo_ref.shape[1]
    ids = column_ids(halo_ref[...], buses)
    edges = ids.shape[1]
    pick_ref[...] = times(theta_ref[...], own_ref[:, :slots])
    lanes = lax.broadcasted_iota(jnp.int32, (edges, buses), 1)
    ids_col = jnp.broadcast_to(ids, (edges, edges)).T[:, :1]
    inner = 1.0 - jnp.max(jnp.where(lanes == ids_col, 1.0, 0.0), axis=0, keepdims=True)
    bus_ids = lax.broadcasted_iota(jnp.int32, (1, buses), 1)
    inner_ids = jnp.where(inner > 0.0, bus_ids, -1)
    all_ids = jnp.concatenate([ids, inner_ids], axis=1)
    counts = jnp.zeros((8, all_ids.shape[1]), F32)
    step = 128
    for start in range(0, branches, step):
        part = slice(start, start + step)
        f_col = jnp.broadcast_to(from_ref[:, part], (step, step)).T[:, :1]
        t_col = jnp.broadcast_to(to_ref[:, part], (step, step)).T[:, :1]
        is_f = jnp.where(f_col == all_ids, 1.0, 0.0)
        is_t = jnp.where(t_col == all_ids, 1.0, 0.0)
        signed = (is_f - is_t).astype(BF16)
        edge_ref[part, :] = signed[:, :edges]
        inner_ref[part, :] = signed[:, edges:]
        ends = (is_f + is_t).reshape(step // 8, 8, all_ids.shape[1])
        counts = counts + jnp.sum(ends, axis=0)
    count = jnp.broadcast_to(jnp.sum(counts, axis=0, keepdims=True), counts.shape)
    count_edge_ref[...] = count[:, :edges]
    count_inner_ref[...] = count[:, edges:]
    x = theta_ref[...] * inner
    x_ref[...] = x
    p = times_t(x, inner_ref[...])
    p_ref[...] = p
    for copy in copies:
        copy.wait()
    weight = stiff_ref[...] * (1.0 - outage_ref[...].astype(F32))
    gain_ref[...] = PENALTY * weight / (PENALTY + 2.0 * weight)
    c_ref[...] = p - (lam_f_ref[...] - lam_t_ref[...]) / PENALTY
    sum_ref[...] = jnp.broadcast_to(jnp.sum(dual_ref[...], axis=0, keepdims=True), sum_ref.shape)
    for index, ref in enumerate((base_ref, load_ref, cost_ref, limit_ref)):
        rows_ref[2 * index : 2 * index + 2, :] = jnp.broadcast_to(ref[...], (2, buses))


def first_kernel(
    far_ref,
    got1_ref,
    pick1_ref,
    edge_ref,
    p_ref,
    c_ref,
    gain_ref,
    count_ref,
    send_ref,
    z_ref,
    delta_ref,
    flow_ref,
):
    slots = pick1_ref.shape[1]
    conts = p_ref.shape[0]
    z = jnp.concatenate([pick1_ref[...] + got1_ref[...], far_ref[...]], axis=1)
    z_ref[...] = z
    moved = times_t(z, edge_ref[...])
    delta_ref[...] = p_ref[...] + moved
    flow = gain_ref[...] * (c_ref[...] + moved)
    flow_ref[...] = flow
    send_ref[:conts, :] = times(flow, edge_ref[:, slots:])
    send_ref[conts:, :] = count_ref[:, slots:]


def both_ends(far_ref, got1_ref, send1_ref, rows):
    return jnp.concatenate(
        [send1_ref[rows, :] + got1_ref[rows, :], far_ref[rows, :]], axis=1
    )


def round_step(
    far_ref, got1_ref, send1_ref, z_ref, degree, edge_ref, p_ref, c_ref, gain_ref, outs
):
    both_ref, z_out_ref, flow_ref, out_ref, *deltas = outs
    slots = out_ref.shape[1]
    both = both_ends(far_ref, got1_ref, send1_ref, slice(0, z_ref.shape[0]))
    both_ref[...] = both
    z = (degree * z_ref[...] - both) / (degree + 1.0)
    z_out_ref[...] = z
    moved = times_t(z, edge_ref[...])
    for delta_ref in deltas:
        delta_ref[...] = p_ref[...] + moved
    flow = gain_ref[...] * (c_ref[...] + 2.0 * moved)
    flow_ref[...] = flow
    out_ref[...] = times(flow, edge_ref[:, slots:])


def second_kernel(
    far_ref, got1_ref, send1_ref, z_ref, edge_ref, p_ref, c_ref, gain_ref, *outs
):
    *outs, degree_ref = outs
    rows = slice(z_ref.shape[0], send1_ref.shape[0])
    degree = both_ends(far_ref, got1_ref, send1_ref, rows)
    degree_ref[...] = degree
    round_step(
        far_ref,
        got1_ref,
        send1_ref,
        z_ref,
        degree[:1, :],
        edge_ref,
        p_ref,
        c_ref,
        gain_ref,
        outs,
    )


def next_kernel(
    far_ref,
    got1_ref,
    send1_ref,
    z_ref,
    degree_ref,
    edge_ref,
    p_ref,
    c_ref,
    gain_ref,
    *outs,
):
    round_step(
        far_ref,
        got1_ref,
        send1_ref,
        z_ref,
        degree_ref[:1, :],
        edge_ref,
        p_ref,
        c_ref,
        gain_ref,
        outs,
    )


def send_kernel(flow_ref, edge_ref, *refs):
    *counts, send_ref = refs
    conts, slots = flow_ref.shape[0], send_ref.shape[1]
    send_ref[:conts, :] = times(flow_ref[...], edge_ref[:, :slots])
    for ref in counts:
        send_ref[conts:, :] = ref[:, :slots]


def inner_step(flow_ref, x_ref, count_ref, inner_ref):
    net = times(flow_ref[...], inner_ref[...])
    count = count_ref[:1, :]
    return net, (count * x_ref[...] - net) / (count + 1.0)


def beside_kernel(
    flow_ref, delta_ref, x_ref, count_ref, inner_ref, net_ref, x_out_ref, p_ref, c_ref
):
    net, x = inner_step(flow_ref, x_ref, count_ref, inner_ref)
    net_ref[...] = net
    x_out_ref[...] = x
    p = times_t(x, inner_ref[...])
    p_ref[...] = p
    c_ref[...] = 2.0 * (p + flow_ref[...]) - delta_ref[...]


def beside_last_kernel(
    flow_ref,
    x_ref,
    count_ref,
    inner_ref,
    own_ref,
    dual_ref,
    rows_ref,
    dsum_ref,
    *refs,
):
    *refs, net_ref, x_out_ref, dual_out_ref, sums_ref = refs
    rounds = len(refs) // 2
    net, x = inner_step(flow_ref, x_ref, count_ref, inner_ref)
    net_ref[...] = net
    x_out_ref[...] = x
    conts = net.shape[0]
    edge = jnp.concatenate([ref[...] for ref in refs[:rounds]], axis=0)
    spread = times_t(edge, own_ref[...])
    part = 1.0 / (rows_ref[4:5, :] + PENALTY + BALANCE)
    dual = dual_ref[...]
    sums_ref[0:1, :] = dsum_ref[:1, :]
    for index, ref in enumerate(refs[rounds:]):
        whole = ref[...] + spread[index * conts : (index + 1) * conts]
        sums_ref[index + 1 : index + 2, :] = jnp.sum(whole, axis=0, keepdims=True)
        dual = dual + part * (BALANCE * whole - dual)
    tail = sums_ref.shape[0] - rounds - 1
    sums_ref[rounds + 1 :, :] = jnp.broadcast_to(
        jnp.sum(net, axis=0, keepdims=True), (tail, net.shape[1])
    )
    dual_out_ref[...] = dual


def total_kernel(
    far_ref, got1_ref, send1_ref, own_ref, sums_in_ref, both_ref, sums_ref
):
    both = both_ends(far_ref, got1_ref, send1_ref, slice(0, send1_ref.shape[0]))
    both_ref[...] = both
    row = jnp.broadcast_to(jnp.sum(both, axis=0, keepdims=True), (8, both.shape[1]))
    sums_ref[...] = sums_in_ref[...]
    last = slice(ROUNDS, ROUNDS + 1)
    sums_ref[last, :] = sums_in_ref[last, :] + times_t(row, own_ref[...])[:1]


def field_kernel(
    both_ref, z_ref, degree_ref, own_ref, x_ref, net_ref, dual_ref, rows_ref, theta_ref, gen_ref
):
    conts = net_ref.shape[0]
    both = both_ref[...]
    degree = degree_ref[:1, :]
    z = (degree * z_ref[...] - both) / (degree + 1.0)
    spread = times_t(jnp.concatenate([both, z], axis=0), own_ref[...])
    theta_ref[...] = x_ref[...] + spread[conts:]
    part = 1.0 / (rows_ref[4:5, :] + PENALTY + BALANCE)
    gen_ref[...] = part * (BALANCE * (net_ref[...] + spread[:conts]) - dual_ref[...])


def end_kernel(contingencies, *refs):
    *sum_refs, rows_ref, part_gen_ref, gen_ref, base_out_ref = refs
    total = sum_refs[0][...]
    for ref in sum_refs[1:]:
        total = total + ref[...]
    mean = total / contingencies
    base, load = rows_ref[0:1, :], rows_ref[2:3, :]
    limit = rows_ref[6:7, :]
    part = 1.0 / (rows_ref[4:5, :] + PENALTY + BALANCE)
    dual_mean = mean[0:1, :]
    shared = jnp.zeros_like(base)
    for index in range(ROUNDS):
        net_mean = mean[index + 1 : index + 2, :]
        gen_shared = part * (PENALTY * base - shared + BALANCE * load)
        if index == ROUNDS - 1:
            gen_ref[...] = part_gen_ref[...] + gen_shared
        gen_mean = part * (PENALTY * base - dual_mean + BALANCE * (load + net_mean))
        dual_mean = dual_mean + PENALTY * (gen_mean - base)
        shared = shared + PENALTY * (gen_shared - base)
        base = jnp.clip(gen_mean + dual_mean / PENALTY, 0.0, limit)
    base_out_ref[...] = base


def call(kernel, outs, *args, scratch=(), spaces=None, flops=2 * 128 * 640 * 512):
    shapes = [jax.ShapeDtypeStruct(shape, dtype) for shape, dtype in outs]
    moved = sum(a.size * a.dtype.itemsize for a in args)
    spaces = spaces or [pltpu.VMEM] * len(args)
    return pl.pallas_call(
        kernel,
        out_shape=shapes,
        in_specs=[pl.BlockSpec(memory_space=space) for space in spaces],
        out_specs=[pl.BlockSpec(memory_space=pltpu.VMEM)] * len(outs),
        scratch_shapes=list(scratch),
        compiler_params=pltpu.CompilerParams(vmem_limit_bytes=32 * 1024 * 1024),
        cost_estimate=pl.CostEstimate(flops=flops, bytes_accessed=moved, transcendentals=0),
    )(*args)


def swaps(conts, nets):
    def pairs(shift):
        found = []
        for c in range(conts):
            for p in range(nets):
                q = p + 1 if p % 2 == shift else p - 1
                if 0 <= q < nets:
                    found.append((c * nets + p, c * nets + q))
                elif (c ^ 1) < conts:
                    found.append((c * nets + p, (c ^ 1) * nets + p))
                else:
                    found.append((c * nets + p, c * nets + p))
        return found

    return pairs(0), pairs(1)


def local(
    angles,
    lam_from,
    lam_to,
    gen_dual,
    base_prev,
    outage,
    from_bus,
    to_ref,
    halo_rows,
    stiffness,
    bus_load,
    gen_cost,
    gen_limit,
):
    conts, buses = angles.shape
    branches = from_bus.shape[0]
    slots = halo_rows.shape[0]
    edges = 2 * slots
    cont_size = lax.axis_size("cont")
    net_size = lax.axis_size("net")
    swap1, swap2 = swaps(cont_size, net_size)
    axes = ("cont", "net")

    def trade_near(value):
        return lax.ppermute(value, axes, swap1)

    def trade_far(value):
        return lax.ppermute(value, axes, swap2)

    def in_hbm(*arrays):
        return [pltpu.with_memory_space_constraint(a, pltpu.HBM) for a in arrays]

    bus = ((conts, buses), F32)
    branch = ((conts, branches), F32)
    half = ((conts, slots), F32)
    edge = ((conts, edges), F32)
    tall = ((conts + 8, slots), F32)
    row = ((8, buses), F32)

    halo_row = halo_rows.reshape(1, slots)
    fetched = [halo_row, angles, from_bus, to_ref, stiffness]
    number = len(fetched)

    def load(*refs):
        load_kernel(number, *refs)

    *here, pick2, own = call(
        load,
        [(a.shape, a.dtype) for a in fetched] + [half, ((buses, edges), BF16)],
        *in_hbm(*fetched),
        spaces=[pltpu.HBM] * number,
        scratch=[pltpu.SemaphoreType.DMA((number,))],
    )
    got2 = trade_far(pick2)
    halo_row, angles = here[:2]
    from_row, to_row, stiff_row = (a.reshape(1, branches) for a in here[2:])
    rows = [a.reshape(1, buses) for a in (base_prev, bus_load, gen_cost, gen_limit)]
    fetched = [lam_from, lam_to, outage, gen_dual, *rows]
    near_args = [angles, from_row, to_row, halo_row, stiff_row, own]
    (
        gen_dual,
        pick1,
        edge_table,
        inner_table,
        gain,
        x,
        p,
        c,
        count_edge,
        count_inner,
        dual_sum,
        rows,
    ) = call(
        prep_kernel,
        [
            bus,
            half,
            ((branches, edges), BF16),
            ((branches, buses), BF16),
            branch,
            bus,
            branch,
            branch,
            ((8, edges), F32),
            row,
            row,
            row,
        ],
        *in_hbm(*fetched),
        *near_args,
        spaces=[pltpu.HBM] * len(fetched) + [pltpu.VMEM] * len(near_args),
        scratch=[pltpu.VMEM(a.shape, a.dtype) for a in (lam_from, lam_to, outage)]
        + [pltpu.VMEM((1, buses), F32)] * 4
        + [pltpu.SemaphoreType.DMA((len(fetched),))],
    )
    got1 = trade_near(pick1)
    send2, z, delta, flow = call(
        first_kernel,
        [tall, edge, branch, branch],
        pick2 + got2,
        got1,
        pick1,
        edge_table,
        p,
        c,
        gain,
        count_edge,
    )
    nets, boths = [], []
    for index in range(1, ROUNDS):
        first = index == 1
        got2 = trade_far(send2)
        counts = [count_edge] if first else []
        (send1,) = call(send_kernel, [tall if first else half], flow, edge_table, *counts)
        got1 = trade_near(send1)
        net, x, p, c = call(
            beside_kernel,
            [bus, bus, branch, branch],
            flow,
            delta,
            x,
            count_inner,
            inner_table,
        )
        nets.append(net)
        outs = [edge, edge, branch, half]
        if index < ROUNDS - 1:
            outs = outs + [branch]
        ends = [send2 + got2, got1, send1, z]
        tables = [edge_table, p, c, gain]
        if first:
            both, z, flow, send2, *deltas, degree = call(
                second_kernel, outs + [((8, edges), F32)], *ends, *tables
            )
        else:
            both, z, flow, send2, *deltas = call(next_kernel, outs, *ends, degree, *tables)
        delta = deltas[0] if deltas else None
        boths.append(both)
    got2 = trade_far(send2)
    (send1,) = call(send_kernel, [half], flow, edge_table)
    got1 = trade_near(send1)
    net, x, dual, sums = call(
        beside_last_kernel,
        [bus, bus, bus, row],
        flow,
        x,
        count_inner,
        inner_table,
        own,
        gen_dual,
        rows,
        dual_sum,
        *boths,
        *nets,
    )
    both, sums = call(total_kernel, [edge, row], send2 + got2, got1, send1, own, sums)
    parts = [sums]
    for shift in range(1, cont_size):
        parts.append(
            lax.ppermute(sums, "cont", [(i, (i + shift) % cont_size) for i in range(cont_size)])
        )

    theta, part_gen = call(
        field_kernel,
        [bus, bus],
        both,
        z,
        degree,
        own,
        x,
        net,
        dual,
        rows,
    )

    def finish(*refs):
        end_kernel(float(conts * cont_size), *refs)

    generation, base = call(finish, [bus, ((1, buses), F32)], *parts, rows, part_gen)
    return theta, generation, base.reshape(buses)


def solution(mesh):
    placed = (
        P("cont", "net"),
        P("cont", "net"),
        P("cont", "net"),
        P("cont", "net"),
        P("net"),
        P("cont", "net"),
        P("net"),
        P("net"),
        P("net"),
        P("net"),
        P("net"),
        P("net"),
        P("net"),
    )
    return jax.shard_map(
        local,
        mesh=mesh,
        in_specs=placed,
        out_specs=(P("cont", "net"), P("cont", "net"), P("net")),
        check_vma=False,
    )
```

```python
import jax
import jax.numpy as jnp
from jax import lax
from jax.experimental import pallas as pl
from jax.experimental.pallas import tpu as pltpu
from jax.sharding import PartitionSpec as P

ROUNDS = 4
PENALTY = 1.0
BALANCE = 2.0
F32 = jnp.float32
BF16 = jnp.bfloat16


def halves(value):
    high = value.astype(BF16)
    low = (value - high.astype(F32)).astype(BF16)
    return jnp.concatenate([high, low], axis=0)


def times(value, table):
    rows = value.shape[0]
    both = jnp.dot(halves(value), table, preferred_element_type=F32)
    return both[:rows] + both[rows:]


def times_t(value, table):
    rows = value.shape[0]
    both = lax.dot_general(
        halves(value), table, (((1,), (1,)), ((), ())), preferred_element_type=F32
    )
    return both[:rows] + both[rows:]


def column_ids(halo_row, buses):
    slots = halo_row.shape[1]
    own = jnp.where(halo_row < buses, halo_row, -1)
    away = buses + lax.broadcasted_iota(jnp.int32, (1, slots), 1)
    even = lax.axis_index("net") % 2 == 0
    first = jnp.where(even, away, own)
    second = jnp.where(even, own, away)
    return jnp.concatenate([first, second], axis=1)


def fetch(sources, targets, semaphores):
    copies = [
        pltpu.make_async_copy(source, target, semaphores.at[index])
        for index, (source, target) in enumerate(zip(sources, targets))
    ]
    for copy in copies:
        copy.start()
    return copies


def load_kernel(count, *refs):
    sources, targets = refs[:count], refs[count : 2 * count]
    pick1_ref, pick2_ref, own_ref, semaphores = refs[2 * count :]
    copies = fetch(sources, targets, semaphores)
    halo_ref, theta_ref = targets[:2]
    buses = theta_ref.shape[1]
    slots = halo_ref.shape[1]
    copies[0].wait()
    ids = column_ids(halo_ref[...], buses)
    rows = lax.broadcasted_iota(jnp.int32, (buses, ids.shape[1]), 0)
    table = jnp.where(rows == ids, 1.0, 0.0).astype(BF16)
    own_ref[...] = table
    copies[1].wait()
    pick = times(theta_ref[...], table)
    pick1_ref[...] = pick[:, :slots]
    pick2_ref[...] = pick[:, slots:]
    for copy in copies[2:]:
        copy.wait()


def prep_kernel(
    lam_f_hbm,
    lam_t_hbm,
    outage_hbm,
    dual_hbm,
    base_hbm,
    load_hbm,
    cost_hbm,
    limit_hbm,
    theta_ref,
    from_ref,
    to_ref,
    halo_ref,
    stiff_ref,
    dual_ref,
    edge_ref,
    inner_ref,
    gain_ref,
    x_ref,
    p_ref,
    c_ref,
    count_edge_ref,
    count_inner_ref,
    sum_ref,
    rows_ref,
    lam_f_ref,
    lam_t_ref,
    outage_ref,
    base_ref,
    load_ref,
    cost_ref,
    limit_ref,
    semaphores,
):
    sources = (
        lam_f_hbm, lam_t_hbm, outage_hbm, dual_hbm, base_hbm, load_hbm, cost_hbm, limit_hbm
    )
    targets = (
        lam_f_ref, lam_t_ref, outage_ref, dual_ref, base_ref, load_ref, cost_ref, limit_ref
    )
    copies = fetch(sources, targets, semaphores)
    buses = theta_ref.shape[1]
    branches = from_ref.shape[1]
    ids = column_ids(halo_ref[...], buses)
    edges = ids.shape[1]
    lanes = lax.broadcasted_iota(jnp.int32, (edges, buses), 1)
    ids_col = jnp.broadcast_to(ids, (edges, edges)).T[:, :1]
    inner = 1.0 - jnp.max(jnp.where(lanes == ids_col, 1.0, 0.0), axis=0, keepdims=True)
    bus_ids = lax.broadcasted_iota(jnp.int32, (1, buses), 1)
    inner_ids = jnp.where(inner > 0.0, bus_ids, -1)
    all_ids = jnp.concatenate([ids, inner_ids], axis=1)
    counts = jnp.zeros((8, all_ids.shape[1]), F32)
    step = 128
    for start in range(0, branches, step):
        part = slice(start, start + step)
        f_col = jnp.broadcast_to(from_ref[:, part], (step, step)).T[:, :1]
        t_col = jnp.broadcast_to(to_ref[:, part], (step, step)).T[:, :1]
        is_f = jnp.where(f_col == all_ids, 1.0, 0.0)
        is_t = jnp.where(t_col == all_ids, 1.0, 0.0)
        signed = (is_f - is_t).astype(BF16)
        edge_ref[part, :] = signed[:, :edges]
        inner_ref[part, :] = signed[:, edges:]
        ends = (is_f + is_t).reshape(step // 8, 8, all_ids.shape[1])
        counts = counts + jnp.sum(ends, axis=0)
    count = jnp.broadcast_to(jnp.sum(counts, axis=0, keepdims=True), counts.shape)
    count_edge_ref[...] = count[:, :edges]
    count_inner_ref[...] = count[:, edges:]
    x = theta_ref[...] * inner
    x_ref[...] = x
    p = times_t(x, inner_ref[...])
    p_ref[...] = p
    for copy in copies:
        copy.wait()
    weight = stiff_ref[...] * (1.0 - outage_ref[...].astype(F32))
    gain_ref[...] = PENALTY * weight / (PENALTY + 2.0 * weight)
    c_ref[...] = p - (lam_f_ref[...] - lam_t_ref[...]) / PENALTY
    sum_ref[...] = jnp.broadcast_to(jnp.sum(dual_ref[...], axis=0, keepdims=True), sum_ref.shape)
    for index, ref in enumerate((base_ref, load_ref, cost_ref, limit_ref)):
        rows_ref[2 * index : 2 * index + 2, :] = jnp.broadcast_to(ref[...], (2, buses))


def gap_step(z, scale, edge_ref, p_ref, c_ref, gain_ref, flow_ref, send_ref, deltas):
    conts, slots = z.shape[0], send_ref.shape[1]
    place, places = lax.axis_index("net"), lax.axis_size("net")
    has_far = jnp.where(place % 2 == 0, place > 0, place < places - 1)

    def finish(moved):
        for delta_ref in deltas:
            delta_ref[...] = p_ref[...] + moved
        flow = gain_ref[...] * (c_ref[...] + scale * moved)
        flow_ref[...] = flow
        return flow

    @pl.when(has_far)
    def _():
        flow = finish(times_t(z, edge_ref[...]))
        send_ref[:conts, :] = times(flow, edge_ref[:, slots:])

    @pl.when(jnp.logical_not(has_far))
    def _():
        finish(times_t(z[:, :slots], edge_ref[:, :slots]))
        send_ref[:conts, :] = jnp.zeros((conts, slots), F32)


def first_kernel(
    far_ref,
    got1_ref,
    pick1_ref,
    edge_ref,
    p_ref,
    c_ref,
    gain_ref,
    count_ref,
    send_ref,
    z_ref,
    delta_ref,
    flow_ref,
):
    slots = pick1_ref.shape[1]
    conts = p_ref.shape[0]
    z = jnp.concatenate([pick1_ref[...] + got1_ref[...], far_ref[...]], axis=1)
    z_ref[...] = z
    gap_step(z, 1.0, edge_ref, p_ref, c_ref, gain_ref, flow_ref, send_ref, [delta_ref])
    send_ref[conts:, :] = count_ref[:, slots:]


def both_ends(far_ref, got1_ref, send1_ref, rows):
    return jnp.concatenate(
        [send1_ref[rows, :] + got1_ref[rows, :], far_ref[rows, :]], axis=1
    )


def round_step(
    far_ref, got1_ref, send1_ref, z_ref, degree, edge_ref, p_ref, c_ref, gain_ref, outs
):
    both_ref, z_out_ref, flow_ref, out_ref, *deltas = outs
    both = both_ends(far_ref, got1_ref, send1_ref, slice(0, z_ref.shape[0]))
    both_ref[...] = both
    z = (degree * z_ref[...] - both) / (degree + 1.0)
    z_out_ref[...] = z
    gap_step(z, 2.0, edge_ref, p_ref, c_ref, gain_ref, flow_ref, out_ref, deltas)


def second_kernel(
    far_ref, got1_ref, send1_ref, z_ref, edge_ref, p_ref, c_ref, gain_ref, *outs
):
    *outs, degree_ref = outs
    rows = slice(z_ref.shape[0], send1_ref.shape[0])
    degree = both_ends(far_ref, got1_ref, send1_ref, rows)
    degree_ref[...] = degree
    round_step(
        far_ref,
        got1_ref,
        send1_ref,
        z_ref,
        degree[:1, :],
        edge_ref,
        p_ref,
        c_ref,
        gain_ref,
        outs,
    )


def next_kernel(
    far_ref,
    got1_ref,
    send1_ref,
    z_ref,
    degree_ref,
    edge_ref,
    p_ref,
    c_ref,
    gain_ref,
    *outs,
):
    round_step(
        far_ref,
        got1_ref,
        send1_ref,
        z_ref,
        degree_ref[:1, :],
        edge_ref,
        p_ref,
        c_ref,
        gain_ref,
        outs,
    )


def send_kernel(flow_ref, edge_ref, *refs):
    *counts, send_ref = refs
    conts, slots = flow_ref.shape[0], send_ref.shape[1]
    send_ref[:conts, :] = times(flow_ref[...], edge_ref[:, :slots])
    for ref in counts:
        send_ref[conts:, :] = ref[:, :slots]


def inner_step(flow_ref, x_ref, count_ref, inner_ref):
    net = times(flow_ref[...], inner_ref[...])
    count = count_ref[:1, :]
    return net, (count * x_ref[...] - net) / (count + 1.0)


def beside_kernel(
    flow_ref, delta_ref, x_ref, count_ref, inner_ref, net_ref, x_out_ref, p_ref, c_ref
):
    net, x = inner_step(flow_ref, x_ref, count_ref, inner_ref)
    net_ref[...] = net
    x_out_ref[...] = x
    p = times_t(x, inner_ref[...])
    p_ref[...] = p
    c_ref[...] = 2.0 * (p + flow_ref[...]) - delta_ref[...]


def beside_last_kernel(
    flow_ref,
    x_ref,
    count_ref,
    inner_ref,
    own_ref,
    dual_ref,
    rows_ref,
    dsum_ref,
    *refs,
):
    *refs, net_ref, x_out_ref, dual_out_ref, sums_ref = refs
    rounds = len(refs) // 2
    net, x = inner_step(flow_ref, x_ref, count_ref, inner_ref)
    net_ref[...] = net
    x_out_ref[...] = x
    conts = net.shape[0]
    edge = jnp.concatenate([ref[...] for ref in refs[:rounds]], axis=0)
    spread = times_t(edge, own_ref[...])
    part = 1.0 / (rows_ref[4:5, :] + PENALTY + BALANCE)
    dual = dual_ref[...]
    sums_ref[0:1, :] = dsum_ref[:1, :]
    for index, ref in enumerate(refs[rounds:]):
        whole = ref[...] + spread[index * conts : (index + 1) * conts]
        sums_ref[index + 1 : index + 2, :] = jnp.sum(whole, axis=0, keepdims=True)
        dual = dual + part * (BALANCE * whole - dual)
    tail = sums_ref.shape[0] - rounds - 1
    sums_ref[rounds + 1 :, :] = jnp.broadcast_to(
        jnp.sum(net, axis=0, keepdims=True), (tail, net.shape[1])
    )
    dual_out_ref[...] = dual


def total_kernel(
    far_ref, got1_ref, send1_ref, own_ref, sums_in_ref, both_ref, sums_ref
):
    both = both_ends(far_ref, got1_ref, send1_ref, slice(0, send1_ref.shape[0]))
    both_ref[...] = both
    row = jnp.broadcast_to(jnp.sum(both, axis=0, keepdims=True), (8, both.shape[1]))
    sums_ref[...] = sums_in_ref[...]
    last = slice(ROUNDS, ROUNDS + 1)
    sums_ref[last, :] = sums_in_ref[last, :] + times_t(row, own_ref[...])[:1]


def field_kernel(
    both_ref, z_ref, degree_ref, own_ref, x_ref, net_ref, dual_ref, rows_ref, theta_ref, gen_ref
):
    conts = net_ref.shape[0]
    both = both_ref[...]
    degree = degree_ref[:1, :]
    z = (degree * z_ref[...] - both) / (degree + 1.0)
    spread = times_t(jnp.concatenate([both, z], axis=0), own_ref[...])
    theta_ref[...] = x_ref[...] + spread[conts:]
    part = 1.0 / (rows_ref[4:5, :] + PENALTY + BALANCE)
    gen_ref[...] = part * (BALANCE * (net_ref[...] + spread[:conts]) - dual_ref[...])


def end_kernel(contingencies, *refs):
    *sum_refs, rows_ref, part_gen_ref, gen_ref, base_out_ref = refs
    total = sum_refs[0][...]
    for ref in sum_refs[1:]:
        total = total + ref[...]
    mean = total / contingencies
    base, load = rows_ref[0:1, :], rows_ref[2:3, :]
    limit = rows_ref[6:7, :]
    part = 1.0 / (rows_ref[4:5, :] + PENALTY + BALANCE)
    dual_mean = mean[0:1, :]
    shared = jnp.zeros_like(base)
    for index in range(ROUNDS):
        net_mean = mean[index + 1 : index + 2, :]
        gen_shared = part * (PENALTY * base - shared + BALANCE * load)
        if index == ROUNDS - 1:
            gen_ref[...] = part_gen_ref[...] + gen_shared
        gen_mean = part * (PENALTY * base - dual_mean + BALANCE * (load + net_mean))
        dual_mean = dual_mean + PENALTY * (gen_mean - base)
        shared = shared + PENALTY * (gen_shared - base)
        base = jnp.clip(gen_mean + dual_mean / PENALTY, 0.0, limit)
    base_out_ref[...] = base


def call(kernel, outs, *args, scratch=(), spaces=None, flops=2 * 128 * 640 * 512):
    shapes = [jax.ShapeDtypeStruct(shape, dtype) for shape, dtype in outs]
    moved = sum(a.size * a.dtype.itemsize for a in args)
    spaces = spaces or [pltpu.VMEM] * len(args)
    return pl.pallas_call(
        kernel,
        out_shape=shapes,
        in_specs=[pl.BlockSpec(memory_space=space) for space in spaces],
        out_specs=[pl.BlockSpec(memory_space=pltpu.VMEM)] * len(outs),
        scratch_shapes=list(scratch),
        compiler_params=pltpu.CompilerParams(vmem_limit_bytes=32 * 1024 * 1024),
        cost_estimate=pl.CostEstimate(flops=flops, bytes_accessed=moved, transcendentals=0),
    )(*args)


def swaps(conts, nets):
    def pairs(shift):
        found = []
        for c in range(conts):
            for p in range(nets):
                q = p + 1 if p % 2 == shift else p - 1
                if 0 <= q < nets:
                    found.append((c * nets + p, c * nets + q))
                elif (c ^ 1) < conts:
                    found.append((c * nets + p, (c ^ 1) * nets + p))
                else:
                    found.append((c * nets + p, c * nets + p))
        return found

    return pairs(0), pairs(1)


def local(
    angles,
    lam_from,
    lam_to,
    gen_dual,
    base_prev,
    outage,
    from_bus,
    to_ref,
    halo_rows,
    stiffness,
    bus_load,
    gen_cost,
    gen_limit,
):
    conts, buses = angles.shape
    branches = from_bus.shape[0]
    slots = halo_rows.shape[0]
    edges = 2 * slots
    cont_size = lax.axis_size("cont")
    net_size = lax.axis_size("net")
    swap1, swap2 = swaps(cont_size, net_size)
    axes = ("cont", "net")

    def trade_near(value):
        return lax.ppermute(value, axes, swap1)

    def trade_far(value):
        return lax.ppermute(value, axes, swap2)

    def in_hbm(*arrays):
        return [pltpu.with_memory_space_constraint(a, pltpu.HBM) for a in arrays]

    bus = ((conts, buses), F32)
    branch = ((conts, branches), F32)
    half = ((conts, slots), F32)
    edge = ((conts, edges), F32)
    tall = ((conts + 8, slots), F32)
    row = ((8, buses), F32)

    halo_row = halo_rows.reshape(1, slots)
    fetched = [halo_row, angles, from_bus, to_ref, stiffness]
    number = len(fetched)

    def load(*refs):
        load_kernel(number, *refs)

    *here, pick1, pick2, own = call(
        load,
        [(a.shape, a.dtype) for a in fetched] + [half, half, ((buses, edges), BF16)],
        *in_hbm(*fetched),
        spaces=[pltpu.HBM] * number,
        scratch=[pltpu.SemaphoreType.DMA((number,))],
    )
    got2 = trade_far(pick2)
    got1 = trade_near(pick1)
    halo_row, angles = here[:2]
    from_row, to_row, stiff_row = (a.reshape(1, branches) for a in here[2:])
    rows = [a.reshape(1, buses) for a in (base_prev, bus_load, gen_cost, gen_limit)]
    fetched = [lam_from, lam_to, outage, gen_dual, *rows]
    near_args = [angles, from_row, to_row, halo_row, stiff_row]
    (
        gen_dual,
        edge_table,
        inner_table,
        gain,
        x,
        p,
        c,
        count_edge,
        count_inner,
        dual_sum,
        rows,
    ) = call(
        prep_kernel,
        [
            bus,
            ((branches, edges), BF16),
            ((branches, buses), BF16),
            branch,
            bus,
            branch,
            branch,
            ((8, edges), F32),
            row,
            row,
            row,
        ],
        *in_hbm(*fetched),
        *near_args,
        spaces=[pltpu.HBM] * len(fetched) + [pltpu.VMEM] * len(near_args),
        scratch=[pltpu.VMEM(a.shape, a.dtype) for a in (lam_from, lam_to, outage)]
        + [pltpu.VMEM((1, buses), F32)] * 4
        + [pltpu.SemaphoreType.DMA((len(fetched),))],
    )
    send2, z, delta, flow = call(
        first_kernel,
        [tall, edge, branch, branch],
        pick2 + got2,
        got1,
        pick1,
        edge_table,
        p,
        c,
        gain,
        count_edge,
    )
    nets, boths = [], []
    for index in range(1, ROUNDS):
        first = index == 1
        got2 = trade_far(send2)
        counts = [count_edge] if first else []
        (send1,) = call(send_kernel, [tall if first else half], flow, edge_table, *counts)
        got1 = trade_near(send1)
        net, x, p, c = call(
            beside_kernel,
            [bus, bus, branch, branch],
            flow,
            delta,
            x,
            count_inner,
            inner_table,
        )
        nets.append(net)
        outs = [edge, edge, branch, half]
        if index < ROUNDS - 1:
            outs = outs + [branch]
        ends = [send2 + got2, got1, send1, z]
        tables = [edge_table, p, c, gain]
        if first:
            both, z, flow, send2, *deltas, degree = call(
                second_kernel, outs + [((8, edges), F32)], *ends, *tables
            )
        else:
            both, z, flow, send2, *deltas = call(next_kernel, outs, *ends, degree, *tables)
        delta = deltas[0] if deltas else None
        boths.append(both)
    got2 = trade_far(send2)
    (send1,) = call(send_kernel, [half], flow, edge_table)
    got1 = trade_near(send1)
    net, x, dual, sums = call(
        beside_last_kernel,
        [bus, bus, bus, row],
        flow,
        x,
        count_inner,
        inner_table,
        own,
        gen_dual,
        rows,
        dual_sum,
        *boths,
        *nets,
    )
    both, sums = call(total_kernel, [edge, row], send2 + got2, got1, send1, own, sums)
    parts = [sums]
    for shift in range(1, cont_size):
        parts.append(
            lax.ppermute(sums, "cont", [(i, (i + shift) % cont_size) for i in range(cont_size)])
        )

    theta, part_gen = call(
        field_kernel,
        [bus, bus],
        both,
        z,
        degree,
        own,
        x,
        net,
        dual,
        rows,
    )

    def finish(*refs):
        end_kernel(float(conts * cont_size), *refs)

    generation, base = call(finish, [bus, ((1, buses), F32)], *parts, rows, part_gen)
    return theta, generation, base.reshape(buses)


def solution(mesh):
    placed = (
        P("cont", "net"),
        P("cont", "net"),
        P("cont", "net"),
        P("cont", "net"),
        P("net"),
        P("cont", "net"),
        P("net"),
        P("net"),
        P("net"),
        P("net"),
        P("net"),
        P("net"),
        P("net"),
    )
    return jax.shard_map(
        local,
        mesh=mesh,
        in_specs=placed,
        out_specs=(P("cont", "net"), P("cont", "net"), P("net")),
        check_vma=False,
    )
```

```python
import jax
import jax.numpy as jnp
from jax import lax
from jax.experimental import pallas as pl
from jax.experimental.pallas import tpu as pltpu
from jax.sharding import PartitionSpec as P

ROUNDS = 4
PENALTY = 1.0
BALANCE = 2.0
F32 = jnp.float32
BF16 = jnp.bfloat16


def halves(value):
    high = value.astype(BF16)
    low = (value - high.astype(F32)).astype(BF16)
    return jnp.concatenate([high, low], axis=0)


def times(value, table):
    rows = value.shape[0]
    both = jnp.dot(halves(value), table, preferred_element_type=F32)
    return both[:rows] + both[rows:]


def times_t(value, table):
    rows = value.shape[0]
    both = lax.dot_general(
        halves(value), table, (((1,), (1,)), ((), ())), preferred_element_type=F32
    )
    return both[:rows] + both[rows:]


def column_ids(halo_row, buses):
    slots = halo_row.shape[1]
    own = jnp.where(halo_row < buses, halo_row, -1)
    away = buses + lax.broadcasted_iota(jnp.int32, (1, slots), 1)
    even = lax.axis_index("net") % 2 == 0
    first = jnp.where(even, away, own)
    second = jnp.where(even, own, away)
    return jnp.concatenate([first, second], axis=1)


def fetch(sources, targets, semaphores):
    copies = [
        pltpu.make_async_copy(source, target, semaphores.at[index])
        for index, (source, target) in enumerate(zip(sources, targets))
    ]
    for copy in copies:
        copy.start()
    return copies


def load_kernel(count, *refs):
    sources, targets = refs[:count], refs[count : 2 * count]
    pick1_ref, pick2_ref, semaphores = refs[2 * count :]
    copies = fetch(sources, targets, semaphores)
    halo_ref, theta_ref = targets[:2]
    buses = theta_ref.shape[1]
    slots = halo_ref.shape[1]
    copies[0].wait()
    ids = column_ids(halo_ref[...], buses)
    rows = lax.broadcasted_iota(jnp.int32, (buses, ids.shape[1]), 0)
    table = jnp.where(rows == ids, 1.0, 0.0).astype(BF16)
    copies[1].wait()
    pick = times(theta_ref[...], table)
    pick1_ref[...] = pick[:, :slots]
    pick2_ref[...] = pick[:, slots:]
    for copy in copies[2:]:
        copy.wait()


def prep_kernel(
    lam_f_hbm,
    lam_t_hbm,
    outage_hbm,
    dual_hbm,
    base_hbm,
    load_hbm,
    cost_hbm,
    limit_hbm,
    theta_ref,
    from_ref,
    to_ref,
    halo_ref,
    stiff_ref,
    dual_ref,
    edge_ref,
    edge_t_ref,
    own_t_ref,
    inner_ref,
    gain_ref,
    x_ref,
    p_ref,
    c_ref,
    count_edge_ref,
    count_inner_ref,
    sum_ref,
    rows_ref,
    lam_f_ref,
    lam_t_ref,
    outage_ref,
    base_ref,
    load_ref,
    cost_ref,
    limit_ref,
    semaphores,
):
    sources = (
        lam_f_hbm, lam_t_hbm, outage_hbm, dual_hbm, base_hbm, load_hbm, cost_hbm, limit_hbm
    )
    targets = (
        lam_f_ref, lam_t_ref, outage_ref, dual_ref, base_ref, load_ref, cost_ref, limit_ref
    )
    copies = fetch(sources, targets, semaphores)
    buses = theta_ref.shape[1]
    branches = from_ref.shape[1]
    ids = column_ids(halo_ref[...], buses)
    edges = ids.shape[1]
    lanes = lax.broadcasted_iota(jnp.int32, (edges, buses), 1)
    ids_col = jnp.broadcast_to(ids, (edges, edges)).T[:, :1]
    own = jnp.where(lanes == ids_col, 1.0, 0.0)
    own_t_ref[...] = own.astype(BF16)
    inner = 1.0 - jnp.max(own, axis=0, keepdims=True)
    starts = jnp.where(ids_col == from_ref[...], 1.0, 0.0)
    edge_t_ref[...] = (starts - jnp.where(ids_col == to_ref[...], 1.0, 0.0)).astype(BF16)
    bus_ids = lax.broadcasted_iota(jnp.int32, (1, buses), 1)
    inner_ids = jnp.where(inner > 0.0, bus_ids, -1)
    all_ids = jnp.concatenate([ids, inner_ids], axis=1)
    counts = jnp.zeros((8, all_ids.shape[1]), F32)
    step = 128
    for start in range(0, branches, step):
        part = slice(start, start + step)
        f_col = jnp.broadcast_to(from_ref[:, part], (step, step)).T[:, :1]
        t_col = jnp.broadcast_to(to_ref[:, part], (step, step)).T[:, :1]
        is_f = jnp.where(f_col == all_ids, 1.0, 0.0)
        is_t = jnp.where(t_col == all_ids, 1.0, 0.0)
        signed = (is_f - is_t).astype(BF16)
        edge_ref[part, :] = signed[:, :edges]
        inner_ref[part, :] = signed[:, edges:]
        ends = (is_f + is_t).reshape(step // 8, 8, all_ids.shape[1])
        counts = counts + jnp.sum(ends, axis=0)
    count = jnp.broadcast_to(jnp.sum(counts, axis=0, keepdims=True), counts.shape)
    count_edge_ref[...] = count[:, :edges]
    count_inner_ref[...] = count[:, edges:]
    x = theta_ref[...] * inner
    x_ref[...] = x
    p = times_t(x, inner_ref[...])
    p_ref[...] = p
    for copy in copies:
        copy.wait()
    weight = stiff_ref[...] * (1.0 - outage_ref[...].astype(F32))
    gain_ref[...] = PENALTY * weight / (PENALTY + 2.0 * weight)
    c_ref[...] = p - (lam_f_ref[...] - lam_t_ref[...]) / PENALTY
    sum_ref[...] = jnp.broadcast_to(jnp.sum(dual_ref[...], axis=0, keepdims=True), sum_ref.shape)
    for index, ref in enumerate((base_ref, load_ref, cost_ref, limit_ref)):
        rows_ref[2 * index : 2 * index + 2, :] = jnp.broadcast_to(ref[...], (2, buses))


def has_far():
    place, places = lax.axis_index("net"), lax.axis_size("net")
    return jnp.where(place % 2 == 0, place > 0, place < places - 1)


def gaps(moved, scale, p_ref, c_ref, gain_ref, flow_ref, deltas):
    for delta_ref in deltas:
        delta_ref[...] = p_ref[...] + moved
    flow = gain_ref[...] * (c_ref[...] + scale * moved)
    flow_ref[...] = flow
    return flow


def gap_step(z, scale, edge_ref, turned_ref, p_ref, c_ref, gain_ref, flow_ref, send_ref, deltas):
    conts, slots = z.shape[0], send_ref.shape[1]

    @pl.when(has_far())
    def _():
        moved = times(z, turned_ref[...])
        flow = gaps(moved, scale, p_ref, c_ref, gain_ref, flow_ref, deltas)
        send_ref[:conts, :] = times(flow, edge_ref[:, slots:])

    @pl.when(jnp.logical_not(has_far()))
    def _():
        send_ref[:conts, :] = jnp.zeros((conts, slots), F32)


def first_kernel(
    far_ref,
    got1_ref,
    pick1_ref,
    edge_ref,
    turned_ref,
    p_ref,
    c_ref,
    gain_ref,
    count_ref,
    send_ref,
    z_ref,
    delta_ref,
    flow_ref,
):
    slots = pick1_ref.shape[1]
    conts = p_ref.shape[0]
    z = jnp.concatenate([pick1_ref[...] + got1_ref[...], far_ref[...]], axis=1)
    z_ref[...] = z
    gap_step(z, 1.0, edge_ref, turned_ref, p_ref, c_ref, gain_ref, flow_ref, send_ref, [delta_ref])
    send_ref[conts:, :] = count_ref[:, slots:]


def both_ends(far_ref, got1_ref, send1_ref, rows):
    return jnp.concatenate(
        [send1_ref[rows, :] + got1_ref[rows, :], far_ref[rows, :]], axis=1
    )


def round_step(
    far_ref, got1_ref, send1_ref, z_ref, degree, edge_ref, turned_ref, p_ref, c_ref, gain_ref, outs
):
    both_ref, z_out_ref, flow_ref, out_ref, *deltas = outs
    both = both_ends(far_ref, got1_ref, send1_ref, slice(0, z_ref.shape[0]))
    both_ref[...] = both
    z = (degree * z_ref[...] - both) / (degree + 1.0)
    z_out_ref[...] = z
    gap_step(z, 2.0, edge_ref, turned_ref, p_ref, c_ref, gain_ref, flow_ref, out_ref, deltas)


def second_kernel(
    far_ref, got1_ref, send1_ref, z_ref, edge_ref, turned_ref, p_ref, c_ref, gain_ref, *outs
):
    *outs, degree_ref = outs
    rows = slice(z_ref.shape[0], send1_ref.shape[0])
    degree = both_ends(far_ref, got1_ref, send1_ref, rows)
    degree_ref[...] = degree
    round_step(
        far_ref,
        got1_ref,
        send1_ref,
        z_ref,
        degree[:1, :],
        edge_ref,
        turned_ref,
        p_ref,
        c_ref,
        gain_ref,
        outs,
    )


def next_kernel(
    far_ref,
    got1_ref,
    send1_ref,
    z_ref,
    degree_ref,
    edge_ref,
    turned_ref,
    p_ref,
    c_ref,
    gain_ref,
    *outs,
):
    round_step(
        far_ref,
        got1_ref,
        send1_ref,
        z_ref,
        degree_ref[:1, :],
        edge_ref,
        turned_ref,
        p_ref,
        c_ref,
        gain_ref,
        outs,
    )


def send_kernel(scale, number, *refs):
    z_ref, edge_ref, turned_ref, p_ref, c_ref, gain_ref, flow_in_ref = refs[:7]
    counts = refs[6 + number : -1 - number]
    outs = refs[-1 - number : -1]
    send_ref = refs[-1]
    conts, slots = z_ref.shape[0], send_ref.shape[1]
    table = edge_ref[:, :slots]

    @pl.when(has_far())
    def _():
        send_ref[:conts, :] = times(flow_in_ref[...], table)

    @pl.when(jnp.logical_not(has_far()))
    def _():
        moved = times(z_ref[:, :slots], turned_ref[:slots, :])
        flow = gaps(moved, scale, p_ref, c_ref, gain_ref, outs[0], outs[1:])
        send_ref[:conts, :] = times(flow, table)

    for ref in counts:
        send_ref[conts:, :] = ref[:, :slots]


def inner_step(flow_ref, x_ref, count_ref, inner_ref):
    net = times(flow_ref[...], inner_ref[...])
    count = count_ref[:1, :]
    return net, (count * x_ref[...] - net) / (count + 1.0)


def beside_kernel(
    flow_ref, delta_ref, x_ref, count_ref, inner_ref, net_ref, x_out_ref, p_ref, c_ref
):
    net, x = inner_step(flow_ref, x_ref, count_ref, inner_ref)
    net_ref[...] = net
    x_out_ref[...] = x
    p = times_t(x, inner_ref[...])
    p_ref[...] = p
    c_ref[...] = 2.0 * (p + flow_ref[...]) - delta_ref[...]


def beside_last_kernel(
    flow_ref,
    x_ref,
    count_ref,
    inner_ref,
    own_ref,
    dual_ref,
    rows_ref,
    dsum_ref,
    *refs,
):
    *refs, net_ref, x_out_ref, dual_out_ref, sums_ref = refs
    rounds = len(refs) // 2
    net, x = inner_step(flow_ref, x_ref, count_ref, inner_ref)
    net_ref[...] = net
    x_out_ref[...] = x
    conts = net.shape[0]
    edge = jnp.concatenate([ref[...] for ref in refs[:rounds]], axis=0)
    spread = times(edge, own_ref[...])
    part = 1.0 / (rows_ref[4:5, :] + PENALTY + BALANCE)
    dual = dual_ref[...]
    sums_ref[0:1, :] = dsum_ref[:1, :]
    for index, ref in enumerate(refs[rounds:]):
        whole = ref[...] + spread[index * conts : (index + 1) * conts]
        sums_ref[index + 1 : index + 2, :] = jnp.sum(whole, axis=0, keepdims=True)
        dual = dual + part * (BALANCE * whole - dual)
    tail = sums_ref.shape[0] - rounds - 1
    sums_ref[rounds + 1 :, :] = jnp.broadcast_to(
        jnp.sum(net, axis=0, keepdims=True), (tail, net.shape[1])
    )
    dual_out_ref[...] = dual


def total_kernel(
    far_ref, got1_ref, send1_ref, own_ref, sums_in_ref, both_ref, sums_ref
):
    both = both_ends(far_ref, got1_ref, send1_ref, slice(0, send1_ref.shape[0]))
    both_ref[...] = both
    row = jnp.broadcast_to(jnp.sum(both, axis=0, keepdims=True), (8, both.shape[1]))
    sums_ref[...] = sums_in_ref[...]
    last = slice(ROUNDS, ROUNDS + 1)
    sums_ref[last, :] = sums_in_ref[last, :] + times(row, own_ref[...])[:1]


def field_kernel(
    both_ref, z_ref, degree_ref, own_ref, x_ref, net_ref, dual_ref, rows_ref, theta_ref, gen_ref
):
    conts = net_ref.shape[0]
    both = both_ref[...]
    degree = degree_ref[:1, :]
    z = (degree * z_ref[...] - both) / (degree + 1.0)
    spread = times(jnp.concatenate([both, z], axis=0), own_ref[...])
    theta_ref[...] = x_ref[...] + spread[conts:]
    part = 1.0 / (rows_ref[4:5, :] + PENALTY + BALANCE)
    gen_ref[...] = part * (BALANCE * (net_ref[...] + spread[:conts]) - dual_ref[...])


def end_kernel(contingencies, *refs):
    *sum_refs, rows_ref, part_gen_ref, gen_ref, base_out_ref = refs
    total = sum_refs[0][...]
    for ref in sum_refs[1:]:
        total = total + ref[...]
    mean = total / contingencies
    base, load = rows_ref[0:1, :], rows_ref[2:3, :]
    limit = rows_ref[6:7, :]
    part = 1.0 / (rows_ref[4:5, :] + PENALTY + BALANCE)
    dual_mean = mean[0:1, :]
    shared = jnp.zeros_like(base)
    for index in range(ROUNDS):
        net_mean = mean[index + 1 : index + 2, :]
        gen_shared = part * (PENALTY * base - shared + BALANCE * load)
        if index == ROUNDS - 1:
            gen_ref[...] = part_gen_ref[...] + gen_shared
        gen_mean = part * (PENALTY * base - dual_mean + BALANCE * (load + net_mean))
        dual_mean = dual_mean + PENALTY * (gen_mean - base)
        shared = shared + PENALTY * (gen_shared - base)
        base = jnp.clip(gen_mean + dual_mean / PENALTY, 0.0, limit)
    base_out_ref[...] = base


def call(kernel, outs, *args, scratch=(), spaces=None, aliases=None, flops=2 * 128 * 640 * 512):
    shapes = [jax.ShapeDtypeStruct(shape, dtype) for shape, dtype in outs]
    moved = sum(a.size * a.dtype.itemsize for a in args)
    spaces = spaces or [pltpu.VMEM] * len(args)
    return pl.pallas_call(
        kernel,
        out_shape=shapes,
        in_specs=[pl.BlockSpec(memory_space=space) for space in spaces],
        out_specs=[pl.BlockSpec(memory_space=pltpu.VMEM)] * len(outs),
        scratch_shapes=list(scratch),
        input_output_aliases=aliases or {},
        compiler_params=pltpu.CompilerParams(vmem_limit_bytes=32 * 1024 * 1024),
        cost_estimate=pl.CostEstimate(flops=flops, bytes_accessed=moved, transcendentals=0),
    )(*args)


def swaps(conts, nets):
    def pairs(shift):
        found = []
        for c in range(conts):
            for p in range(nets):
                q = p + 1 if p % 2 == shift else p - 1
                if 0 <= q < nets:
                    found.append((c * nets + p, c * nets + q))
                elif (c ^ 1) < conts:
                    found.append((c * nets + p, (c ^ 1) * nets + p))
                else:
                    found.append((c * nets + p, c * nets + p))
        return found

    return pairs(0), pairs(1)


def local(
    angles,
    lam_from,
    lam_to,
    gen_dual,
    base_prev,
    outage,
    from_bus,
    to_ref,
    halo_rows,
    stiffness,
    bus_load,
    gen_cost,
    gen_limit,
):
    conts, buses = angles.shape
    branches = from_bus.shape[0]
    slots = halo_rows.shape[0]
    edges = 2 * slots
    cont_size = lax.axis_size("cont")
    net_size = lax.axis_size("net")
    swap1, swap2 = swaps(cont_size, net_size)
    axes = ("cont", "net")

    def trade_near(value):
        return lax.ppermute(value, axes, swap1)

    def trade_far(value):
        return lax.ppermute(value, axes, swap2)

    def in_hbm(*arrays):
        return [pltpu.with_memory_space_constraint(a, pltpu.HBM) for a in arrays]

    bus = ((conts, buses), F32)
    branch = ((conts, branches), F32)
    half = ((conts, slots), F32)
    edge = ((conts, edges), F32)
    tall = ((conts + 8, slots), F32)
    row = ((8, buses), F32)

    halo_row = halo_rows.reshape(1, slots)
    fetched = [halo_row, angles, from_bus, to_ref, stiffness]
    number = len(fetched)

    def load(*refs):
        load_kernel(number, *refs)

    *here, pick1, pick2 = call(
        load,
        [(a.shape, a.dtype) for a in fetched] + [half, half],
        *in_hbm(*fetched),
        spaces=[pltpu.HBM] * number,
        scratch=[pltpu.SemaphoreType.DMA((number,))],
    )
    got2 = trade_far(pick2)
    got1 = trade_near(pick1)
    halo_row, angles = here[:2]
    from_row, to_row, stiff_row = (a.reshape(1, branches) for a in here[2:])
    rows = [a.reshape(1, buses) for a in (base_prev, bus_load, gen_cost, gen_limit)]
    fetched = [lam_from, lam_to, outage, gen_dual, *rows]
    near_args = [angles, from_row, to_row, halo_row, stiff_row]
    (
        gen_dual,
        edge_table,
        edge_turned,
        own,
        inner_table,
        gain,
        x,
        p,
        c,
        count_edge,
        count_inner,
        dual_sum,
        rows,
    ) = call(
        prep_kernel,
        [
            bus,
            ((branches, edges), BF16),
            ((edges, branches), BF16),
            ((edges, buses), BF16),
            ((branches, buses), BF16),
            branch,
            bus,
            branch,
            branch,
            ((8, edges), F32),
            row,
            row,
            row,
        ],
        *in_hbm(*fetched),
        *near_args,
        spaces=[pltpu.HBM] * len(fetched) + [pltpu.VMEM] * len(near_args),
        scratch=[pltpu.VMEM(a.shape, a.dtype) for a in (lam_from, lam_to, outage)]
        + [pltpu.VMEM((1, buses), F32)] * 4
        + [pltpu.SemaphoreType.DMA((len(fetched),))],
    )
    send2, z, delta, flow = call(
        first_kernel,
        [tall, edge, branch, branch],
        pick2 + got2,
        got1,
        pick1,
        edge_table,
        edge_turned,
        p,
        c,
        gain,
        count_edge,
    )
    nets, boths = [], []

    def make_near(first, held, z, p, c, counts):
        def kernel(*refs):
            send_kernel(1.0 if first else 2.0, len(held), *refs)

        args = [z, edge_table, edge_turned, p, c, gain, *held, *counts]
        return call(
            kernel,
            [branch] * len(held) + [tall if first else half],
            *args,
            aliases={6 + index: index for index in range(len(held))},
        )

    for index in range(1, ROUNDS):
        first = index == 1
        got2 = trade_far(send2)
        counts = [count_edge] if first else []
        flow, delta, send1 = make_near(first, [flow, delta], z, p, c, counts)
        got1 = trade_near(send1)
        net, x, p, c = call(
            beside_kernel,
            [bus, bus, branch, branch],
            flow,
            delta,
            x,
            count_inner,
            inner_table,
        )
        nets.append(net)
        outs = [edge, edge, branch, half]
        if index < ROUNDS - 1:
            outs = outs + [branch]
        ends = [send2 + got2, got1, send1, z]
        tables = [edge_table, edge_turned, p, c, gain]
        if first:
            both, z, flow, send2, *deltas, degree = call(
                second_kernel, outs + [((8, edges), F32)], *ends, *tables
            )
        else:
            both, z, flow, send2, *deltas = call(next_kernel, outs, *ends, degree, *tables)
        delta = deltas[0] if deltas else None
        boths.append(both)
    got2 = trade_far(send2)
    flow, send1 = make_near(False, [flow], z, p, c, [])
    got1 = trade_near(send1)
    net, x, dual, sums = call(
        beside_last_kernel,
        [bus, bus, bus, row],
        flow,
        x,
        count_inner,
        inner_table,
        own,
        gen_dual,
        rows,
        dual_sum,
        *boths,
        *nets,
    )
    both, sums = call(total_kernel, [edge, row], send2 + got2, got1, send1, own, sums)
    parts = [sums]
    for shift in reversed(range(1, cont_size)):
        parts.append(
            lax.ppermute(sums, "cont", [(i, (i + shift) % cont_size) for i in range(cont_size)])
        )

    theta, part_gen = call(
        field_kernel,
        [bus, bus],
        both,
        z,
        degree,
        own,
        x,
        net,
        dual,
        rows,
    )

    def finish(*refs):
        end_kernel(float(conts * cont_size), *refs)

    generation, base = call(finish, [bus, ((1, buses), F32)], *parts, rows, part_gen)
    return theta, generation, base.reshape(buses)


def solution(mesh):
    placed = (
        P("cont", "net"),
        P("cont", "net"),
        P("cont", "net"),
        P("cont", "net"),
        P("net"),
        P("cont", "net"),
        P("net"),
        P("net"),
        P("net"),
        P("net"),
        P("net"),
        P("net"),
        P("net"),
    )
    return jax.shard_map(
        local,
        mesh=mesh,
        in_specs=placed,
        out_specs=(P("cont", "net"), P("cont", "net"), P("net")),
        check_vma=False,
    )
```

```python
import jax
import jax.numpy as jnp
from jax import lax
from jax.experimental import pallas as pl
from jax.experimental.pallas import tpu as pltpu
from jax.sharding import PartitionSpec as P

ROUNDS = 4
PENALTY = 1.0
BALANCE = 2.0
F32 = jnp.float32
BF16 = jnp.bfloat16


def halves(value):
    high = value.astype(BF16)
    low = (value - high.astype(F32)).astype(BF16)
    return jnp.concatenate([high, low], axis=0)


def times(value, table):
    rows = value.shape[0]
    both = jnp.dot(halves(value), table, preferred_element_type=F32)
    return both[:rows] + both[rows:]


def times_t(value, table):
    rows = value.shape[0]
    both = lax.dot_general(
        halves(value), table, (((1,), (1,)), ((), ())), preferred_element_type=F32
    )
    return both[:rows] + both[rows:]


def column_ids(halo_row, buses):
    slots = halo_row.shape[1]
    own = jnp.where(halo_row < buses, halo_row, -1)
    away = buses + lax.broadcasted_iota(jnp.int32, (1, slots), 1)
    even = lax.axis_index("net") % 2 == 0
    first = jnp.where(even, away, own)
    second = jnp.where(even, own, away)
    return jnp.concatenate([first, second], axis=1)


def fetch(sources, targets, semaphores):
    copies = [
        pltpu.make_async_copy(source, target, semaphores.at[index])
        for index, (source, target) in enumerate(zip(sources, targets))
    ]
    for copy in copies:
        copy.start()
    return copies


def load_kernel(count, *refs):
    sources, targets = refs[:count], refs[count : 2 * count]
    pick1_ref, pick2_ref, table_ref, semaphores = refs[2 * count :]
    place = lax.axis_index("net")

    @pl.when(place == 0)
    def _():
        pick1_ref[...] = jnp.zeros_like(pick1_ref)
        pick2_ref[...] = jnp.zeros_like(pick2_ref)

    @pl.when(place > 0)
    def _():
        copies = fetch(sources, targets, semaphores)
        halo_ref, theta_ref = targets[:2]
        buses, edges = table_ref.shape
        copies[0].wait()
        ids = column_ids(halo_ref[...], buses)
        rows = lax.broadcasted_iota(jnp.int32, (buses, edges), 0)
        table_ref[...] = jnp.where(rows == ids, 1.0, 0.0).astype(BF16)
        copies[1].wait()
        pick = times(theta_ref[...], table_ref[...])
        pick1_ref[...] = pick[:, : edges // 2]
        pick2_ref[...] = pick[:, edges // 2 :]
        for copy in copies[2:]:
            copy.wait()


def late_kernel(count, *refs):
    sources, semaphores = refs[:count], refs[-1]
    targets = refs[2 * count + 1 : 3 * count + 1]

    @pl.when(lax.axis_index("net") == 0)
    def _():
        for copy in fetch(sources, targets, semaphores):
            copy.wait()


def tables(refs, theta_ref, halo_ref, from_ref, to_ref):
    (
        edge_ref,
        edge_t_ref,
        own_t_ref,
        inner_ref,
        x_ref,
        p_ref,
        count_edge_ref,
        count_inner_ref,
    ) = refs
    buses = theta_ref.shape[1]
    branches = from_ref.shape[1]
    ids = column_ids(halo_ref[...], buses)
    edges = ids.shape[1]
    lanes = lax.broadcasted_iota(jnp.int32, (edges, buses), 1)
    ids_col = jnp.broadcast_to(ids, (edges, edges)).T[:, :1]
    own = jnp.where(lanes == ids_col, 1.0, 0.0)
    own_t_ref[...] = own.astype(BF16)
    inner = 1.0 - jnp.max(own, axis=0, keepdims=True)
    starts = jnp.where(ids_col == from_ref[...], 1.0, 0.0)
    edge_t_ref[...] = (starts - jnp.where(ids_col == to_ref[...], 1.0, 0.0)).astype(BF16)
    bus_ids = lax.broadcasted_iota(jnp.int32, (1, buses), 1)
    inner_ids = jnp.where(inner > 0.0, bus_ids, -1)
    all_ids = jnp.concatenate([ids, inner_ids], axis=1)
    counts = jnp.zeros((8, all_ids.shape[1]), F32)
    step = 128
    for start in range(0, branches, step):
        part = slice(start, start + step)
        f_col = jnp.broadcast_to(from_ref[:, part], (step, step)).T[:, :1]
        t_col = jnp.broadcast_to(to_ref[:, part], (step, step)).T[:, :1]
        is_f = jnp.where(f_col == all_ids, 1.0, 0.0)
        is_t = jnp.where(t_col == all_ids, 1.0, 0.0)
        signed = (is_f - is_t).astype(BF16)
        edge_ref[part, :] = signed[:, :edges]
        inner_ref[part, :] = signed[:, edges:]
        ends = (is_f + is_t).reshape(step // 8, 8, all_ids.shape[1])
        counts = counts + jnp.sum(ends, axis=0)
    count = jnp.broadcast_to(jnp.sum(counts, axis=0, keepdims=True), counts.shape)
    count_edge_ref[...] = count[:, :edges]
    count_inner_ref[...] = count[:, edges:]
    x = theta_ref[...] * inner
    x_ref[...] = x
    p_ref[...] = times_t(x, inner_ref[...])


def prep_kernel(number, *refs):
    sources, refs = refs[:number], refs[number:]
    theta_ref, halo_ref, from_ref, to_ref, stiff_ref = refs[:5]
    dual_ref, gain_ref, c_ref, rows_ref = refs[5:9]
    outs = refs[9:17]
    targets, semaphores = (*refs[17:-1], dual_ref), refs[-1]
    copies = fetch(sources, targets, semaphores)
    lam_f_ref, lam_t_ref, outage_ref = targets[:3]
    per_bus = targets[3:7]

    @pl.when(lax.axis_index("net") >= 0)
    def _():
        tables(outs, theta_ref, halo_ref, from_ref, to_ref)

    for copy in copies:
        copy.wait()
    p_ref = outs[5]
    weight = stiff_ref[...] * (1.0 - outage_ref[...].astype(F32))
    gain_ref[...] = PENALTY * weight / (PENALTY + 2.0 * weight)
    c_ref[...] = p_ref[...] - (lam_f_ref[...] - lam_t_ref[...]) / PENALTY
    for index, ref in enumerate(per_bus):
        rows_ref[2 * index : 2 * index + 2, :] = jnp.broadcast_to(
            ref[...], (2, rows_ref.shape[1])
        )


def has_far():
    place, places = lax.axis_index("net"), lax.axis_size("net")
    return jnp.where(place % 2 == 0, place > 0, place < places - 1)


def gaps(moved, scale, p_ref, c_ref, gain_ref, flow_ref, deltas):
    for delta_ref in deltas:
        delta_ref[...] = p_ref[...] + moved
    flow = gain_ref[...] * (c_ref[...] + scale * moved)
    flow_ref[...] = flow
    return flow


def gap_step(z, scale, edge_ref, turned_ref, p_ref, c_ref, gain_ref, flow_ref, send_ref, deltas):
    conts, slots = z.shape[0], send_ref.shape[1]

    @pl.when(has_far())
    def _():
        moved = times(z, turned_ref[...])
        flow = gaps(moved, scale, p_ref, c_ref, gain_ref, flow_ref, deltas)
        send_ref[:conts, :] = times(flow, edge_ref[:, slots:])

    @pl.when(jnp.logical_not(has_far()))
    def _():
        send_ref[:conts, :] = jnp.zeros((conts, slots), F32)


def first_kernel(
    far_ref,
    got1_ref,
    pick1_ref,
    edge_ref,
    turned_ref,
    p_ref,
    c_ref,
    gain_ref,
    count_ref,
    send_ref,
    z_ref,
    delta_ref,
    flow_ref,
):
    slots = pick1_ref.shape[1]
    conts = p_ref.shape[0]
    z = jnp.concatenate([pick1_ref[...] + got1_ref[...], far_ref[...]], axis=1)
    z_ref[...] = z
    gap_step(z, 1.0, edge_ref, turned_ref, p_ref, c_ref, gain_ref, flow_ref, send_ref, [delta_ref])
    send_ref[conts:, :] = count_ref[:, slots:]


def both_ends(far_ref, got1_ref, send1_ref, rows):
    return jnp.concatenate(
        [send1_ref[rows, :] + got1_ref[rows, :], far_ref[rows, :]], axis=1
    )


def round_step(
    far_ref, got1_ref, send1_ref, z_ref, degree, edge_ref, turned_ref, p_ref, c_ref, gain_ref, outs
):
    both_ref, z_out_ref, flow_ref, out_ref, *deltas = outs
    both = both_ends(far_ref, got1_ref, send1_ref, slice(0, z_ref.shape[0]))
    both_ref[...] = both
    z = (degree * z_ref[...] - both) / (degree + 1.0)
    z_out_ref[...] = z
    gap_step(z, 2.0, edge_ref, turned_ref, p_ref, c_ref, gain_ref, flow_ref, out_ref, deltas)


def second_kernel(
    far_ref, got1_ref, send1_ref, z_ref, edge_ref, turned_ref, p_ref, c_ref, gain_ref, *outs
):
    *outs, degree_ref = outs
    rows = slice(z_ref.shape[0], send1_ref.shape[0])
    degree = both_ends(far_ref, got1_ref, send1_ref, rows)
    degree_ref[...] = degree
    round_step(
        far_ref,
        got1_ref,
        send1_ref,
        z_ref,
        degree[:1, :],
        edge_ref,
        turned_ref,
        p_ref,
        c_ref,
        gain_ref,
        outs,
    )


def next_kernel(
    far_ref,
    got1_ref,
    send1_ref,
    z_ref,
    degree_ref,
    edge_ref,
    turned_ref,
    p_ref,
    c_ref,
    gain_ref,
    *outs,
):
    round_step(
        far_ref,
        got1_ref,
        send1_ref,
        z_ref,
        degree_ref[:1, :],
        edge_ref,
        turned_ref,
        p_ref,
        c_ref,
        gain_ref,
        outs,
    )


def send_kernel(scale, number, *refs):
    z_ref, edge_ref, turned_ref, p_ref, c_ref, gain_ref, flow_in_ref = refs[:7]
    counts = refs[6 + number : -1 - number]
    outs = refs[-1 - number : -1]
    send_ref = refs[-1]
    conts, slots = z_ref.shape[0], send_ref.shape[1]
    table = edge_ref[:, :slots]

    @pl.when(has_far())
    def _():
        send_ref[:conts, :] = times(flow_in_ref[...], table)

    @pl.when(jnp.logical_not(has_far()))
    def _():
        moved = times(z_ref[:, :slots], turned_ref[:slots, :])
        flow = gaps(moved, scale, p_ref, c_ref, gain_ref, outs[0], outs[1:])
        send_ref[:conts, :] = times(flow, table)

    for ref in counts:
        send_ref[conts:, :] = ref[:, :slots]


def inner_step(flow_ref, x_ref, count_ref, inner_ref):
    net = times(flow_ref[...], inner_ref[...])
    count = count_ref[:1, :]
    return net, (count * x_ref[...] - net) / (count + 1.0)


def beside_kernel(
    flow_ref, delta_ref, x_ref, count_ref, inner_ref, net_ref, x_out_ref, p_ref, c_ref
):
    net, x = inner_step(flow_ref, x_ref, count_ref, inner_ref)
    net_ref[...] = net
    x_out_ref[...] = x
    p = times_t(x, inner_ref[...])
    p_ref[...] = p
    c_ref[...] = 2.0 * (p + flow_ref[...]) - delta_ref[...]


def beside_last_kernel(
    flow_ref,
    x_ref,
    count_ref,
    inner_ref,
    own_ref,
    dual_ref,
    rows_ref,
    *refs,
):
    *refs, net_ref, x_out_ref, dual_out_ref, sums_ref = refs
    rounds = len(refs) // 2
    net, x = inner_step(flow_ref, x_ref, count_ref, inner_ref)
    net_ref[...] = net
    x_out_ref[...] = x
    conts = net.shape[0]
    edge = jnp.concatenate([ref[...] for ref in refs[:rounds]], axis=0)
    spread = times(edge, own_ref[...])
    part = 1.0 / (rows_ref[4:5, :] + PENALTY + BALANCE)
    dual = dual_ref[...]
    wholes = [
        ref[...] + spread[index * conts : (index + 1) * conts]
        for index, ref in enumerate(refs[rounds:])
    ]
    for index, whole in enumerate([*wholes, net]):
        term = 2.0 * part * (BALANCE * whole - dual) + dual
        sums_ref[index : index + 1, :] = jnp.sum(term, axis=0, keepdims=True)
        if index < rounds:
            dual = dual + part * (BALANCE * whole - dual)
    dual_out_ref[...] = dual


def total_kernel(
    far_ref, got1_ref, send1_ref, own_ref, rows_ref, sums_in_ref, both_ref, sums_ref
):
    both = both_ends(far_ref, got1_ref, send1_ref, slice(0, send1_ref.shape[0]))
    both_ref[...] = both
    row = jnp.broadcast_to(jnp.sum(both, axis=0, keepdims=True), (8, both.shape[1]))
    sums_ref[...] = sums_in_ref[...]
    last = slice(ROUNDS - 1, ROUNDS)
    part = 1.0 / (rows_ref[4:5, :] + PENALTY + BALANCE)
    late = times(row, own_ref[...])[:1]
    sums_ref[last, :] = sums_in_ref[last, :] + 2.0 * BALANCE * part * late


def field_kernel(
    both_ref, z_ref, degree_ref, own_ref, x_ref, net_ref, dual_ref, rows_ref, theta_ref, gen_ref
):
    conts = net_ref.shape[0]
    both = both_ref[...]
    degree = degree_ref[:1, :]
    z = (degree * z_ref[...] - both) / (degree + 1.0)
    spread = times(jnp.concatenate([both, z], axis=0), own_ref[...])
    theta_ref[...] = x_ref[...] + spread[conts:]
    part = 1.0 / (rows_ref[4:5, :] + PENALTY + BALANCE)
    gen_ref[...] = part * (BALANCE * (net_ref[...] + spread[:conts]) - dual_ref[...])


def end_kernel(contingencies, *refs):
    *sum_refs, rows_ref, part_gen_ref, gen_ref, base_out_ref = refs
    total = sum_refs[0][...]
    for ref in sum_refs[1:]:
        total = total + ref[...]
    mean = total / contingencies
    base, load = rows_ref[0:1, :], rows_ref[2:3, :]
    limit = rows_ref[6:7, :]
    part = 1.0 / (rows_ref[4:5, :] + PENALTY + BALANCE)
    shared = jnp.zeros_like(base)
    for index in range(ROUNDS):
        gen_shared = part * (PENALTY * base - shared + BALANCE * load)
        if index == ROUNDS - 1:
            gen_ref[...] = part_gen_ref[...] + gen_shared
        total_mean = mean[index : index + 1, :] + 2.0 * gen_shared + shared - base
        shared = shared + PENALTY * (gen_shared - base)
        base = jnp.clip(total_mean, 0.0, limit)
    base_out_ref[...] = base


def call(kernel, outs, *args, scratch=(), spaces=None, aliases=None, flops=2 * 128 * 640 * 512):
    shapes = [jax.ShapeDtypeStruct(shape, dtype) for shape, dtype in outs]
    moved = sum(a.size * a.dtype.itemsize for a in args)
    spaces = spaces or [pltpu.VMEM] * len(args)
    return pl.pallas_call(
        kernel,
        out_shape=shapes,
        in_specs=[pl.BlockSpec(memory_space=space) for space in spaces],
        out_specs=[pl.BlockSpec(memory_space=pltpu.VMEM)] * len(outs),
        scratch_shapes=list(scratch),
        input_output_aliases=aliases or {},
        compiler_params=pltpu.CompilerParams(vmem_limit_bytes=32 * 1024 * 1024),
        cost_estimate=pl.CostEstimate(flops=flops, bytes_accessed=moved, transcendentals=0),
    )(*args)


def swaps(conts, nets):
    def pairs(shift):
        found = []
        for c in range(conts):
            for p in range(nets):
                q = p + 1 if p % 2 == shift else p - 1
                if 0 <= q < nets:
                    found.append((c * nets + p, c * nets + q))
                elif (c ^ 1) < conts:
                    found.append((c * nets + p, (c ^ 1) * nets + p))
                else:
                    found.append((c * nets + p, c * nets + p))
        return found

    return pairs(0), pairs(1)


def local(
    angles,
    lam_from,
    lam_to,
    gen_dual,
    base_prev,
    outage,
    from_bus,
    to_ref,
    halo_rows,
    stiffness,
    bus_load,
    gen_cost,
    gen_limit,
):
    conts, buses = angles.shape
    branches = from_bus.shape[0]
    slots = halo_rows.shape[0]
    edges = 2 * slots
    cont_size = lax.axis_size("cont")
    net_size = lax.axis_size("net")
    swap1, swap2 = swaps(cont_size, net_size)
    axes = ("cont", "net")

    def trade_near(value):
        return lax.ppermute(value, axes, swap1)

    def trade_far(value):
        return lax.ppermute(value, axes, swap2)

    def in_hbm(*arrays):
        return [pltpu.with_memory_space_constraint(a, pltpu.HBM) for a in arrays]

    bus = ((conts, buses), F32)
    branch = ((conts, branches), F32)
    half = ((conts, slots), F32)
    edge = ((conts, edges), F32)
    tall = ((conts + 8, slots), F32)
    row = ((8, buses), F32)
    total = ((ROUNDS, buses), F32)

    halo_row = halo_rows.reshape(1, slots)
    fetched = [halo_row, angles, from_bus, to_ref, stiffness]
    count = len(fetched)

    def load(*refs):
        load_kernel(count, *refs)

    def late(*refs):
        late_kernel(count, *refs)

    arrived = [(a.shape, a.dtype) for a in fetched]
    *here, pick1, pick2 = call(
        load,
        arrived + [half, half],
        *in_hbm(*fetched),
        spaces=[pltpu.HBM] * count,
        scratch=[pltpu.VMEM((buses, edges), BF16), pltpu.SemaphoreType.DMA((count,))],
    )
    got2 = trade_far(pick2)
    *here, pick1 = call(
        late,
        arrived + [half],
        *in_hbm(*fetched),
        *here,
        pick1,
        spaces=[pltpu.HBM] * count + [pltpu.VMEM] * (count + 1),
        scratch=[pltpu.SemaphoreType.DMA((count,))],
        aliases={count + index: index for index in range(count + 1)},
    )
    got1 = trade_near(pick1)
    halo_row, angles = here[:2]
    from_row, to_row, stiff_row = (a.reshape(1, branches) for a in here[2:])
    rows = [a.reshape(1, buses) for a in (base_prev, bus_load, gen_cost, gen_limit)]
    fetched = [lam_from, lam_to, outage, *rows, gen_dual]
    near_args = [angles, halo_row, from_row, to_row, stiff_row]
    number = len(fetched)

    def prep(*refs):
        prep_kernel(number, *refs)

    (
        gen_dual,
        gain,
        c,
        rows,
        edge_table,
        edge_turned,
        own,
        inner_table,
        x,
        p,
        count_edge,
        count_inner,
    ) = call(
        prep,
        [
            bus,
            branch,
            branch,
            row,
            ((branches, edges), BF16),
            ((edges, branches), BF16),
            ((edges, buses), BF16),
            ((branches, buses), BF16),
            bus,
            branch,
            ((8, edges), F32),
            row,
        ],
        *in_hbm(*fetched),
        *near_args,
        spaces=[pltpu.HBM] * number + [pltpu.VMEM] * len(near_args),
        scratch=[pltpu.VMEM(a.shape, a.dtype) for a in fetched[:-1]]
        + [pltpu.SemaphoreType.DMA((number,))],
    )
    send2, z, delta, flow = call(
        first_kernel,
        [tall, edge, branch, branch],
        pick2 + got2,
        got1,
        pick1,
        edge_table,
        edge_turned,
        p,
        c,
        gain,
        count_edge,
    )
    nets, boths = [], []

    def make_near(first, held, z, p, c, counts):
        def kernel(*refs):
            send_kernel(1.0 if first else 2.0, len(held), *refs)

        args = [z, edge_table, edge_turned, p, c, gain, *held, *counts]
        return call(
            kernel,
            [branch] * len(held) + [tall if first else half],
            *args,
            aliases={6 + index: index for index in range(len(held))},
        )

    for index in range(1, ROUNDS):
        first = index == 1
        got2 = trade_far(send2)
        counts = [count_edge] if first else []
        flow, delta, send1 = make_near(first, [flow, delta], z, p, c, counts)
        got1 = trade_near(send1)
        net, x, p, c = call(
            beside_kernel,
            [bus, bus, branch, branch],
            flow,
            delta,
            x,
            count_inner,
            inner_table,
        )
        nets.append(net)
        outs = [edge, edge, branch, half]
        if index < ROUNDS - 1:
            outs = outs + [branch]
        ends = [send2 + got2, got1, send1, z]
        tables = [edge_table, edge_turned, p, c, gain]
        if first:
            both, z, flow, send2, *deltas, degree = call(
                second_kernel, outs + [((8, edges), F32)], *ends, *tables
            )
        else:
            both, z, flow, send2, *deltas = call(next_kernel, outs, *ends, degree, *tables)
        delta = deltas[0] if deltas else None
        boths.append(both)
    got2 = trade_far(send2)
    flow, send1 = make_near(False, [flow], z, p, c, [])
    got1 = trade_near(send1)
    net, x, dual, sums = call(
        beside_last_kernel,
        [bus, bus, bus, total],
        flow,
        x,
        count_inner,
        inner_table,
        own,
        gen_dual,
        rows,
        *boths,
        *nets,
    )
    both, sums = call(
        total_kernel, [edge, total], send2 + got2, got1, send1, own, rows, sums
    )
    parts = [sums]
    for shift in reversed(range(1, cont_size)):
        parts.append(
            lax.ppermute(sums, "cont", [(i, (i + shift) % cont_size) for i in range(cont_size)])
        )

    theta, part_gen = call(
        field_kernel,
        [bus, bus],
        both,
        z,
        degree,
        own,
        x,
        net,
        dual,
        rows,
    )

    def finish(*refs):
        end_kernel(float(conts * cont_size), *refs)

    generation, base = call(finish, [bus, ((1, buses), F32)], *parts, rows, part_gen)
    return theta, generation, base.reshape(buses)


def solution(mesh):
    placed = (
        P("cont", "net"),
        P("cont", "net"),
        P("cont", "net"),
        P("cont", "net"),
        P("net"),
        P("cont", "net"),
        P("net"),
        P("net"),
        P("net"),
        P("net"),
        P("net"),
        P("net"),
        P("net"),
    )
    return jax.shard_map(
        local,
        mesh=mesh,
        in_specs=placed,
        out_specs=(P("cont", "net"), P("cont", "net"), P("net")),
        check_vma=False,
    )
```

```python
import jax
import jax.numpy as jnp
from jax import lax
from jax.experimental import pallas as pl
from jax.experimental.pallas import tpu as pltpu
from jax.sharding import PartitionSpec as P

ROUNDS = 4
PENALTY = 1.0
BALANCE = 2.0
F32 = jnp.float32
BF16 = jnp.bfloat16


def halves(value):
    high = value.astype(BF16)
    low = (value - high.astype(F32)).astype(BF16)
    return jnp.concatenate([high, low], axis=0)


def times(value, table):
    rows = value.shape[0]
    both = jnp.dot(halves(value), table, preferred_element_type=F32)
    return both[:rows] + both[rows:]


def times_t(value, table):
    rows = value.shape[0]
    both = lax.dot_general(
        halves(value), table, (((1,), (1,)), ((), ())), preferred_element_type=F32
    )
    return both[:rows] + both[rows:]


def column_ids(halo_row, buses):
    slots = halo_row.shape[1]
    own = jnp.where(halo_row < buses, halo_row, -1)
    away = buses + lax.broadcasted_iota(jnp.int32, (1, slots), 1)
    even = lax.axis_index("net") % 2 == 0
    first = jnp.where(even, away, own)
    second = jnp.where(even, own, away)
    return jnp.concatenate([first, second], axis=1)


def fetch(sources, targets, semaphores):
    copies = [
        pltpu.make_async_copy(source, target, semaphores.at[index])
        for index, (source, target) in enumerate(zip(sources, targets))
    ]
    for copy in copies:
        copy.start()
    return copies


def load_kernel(count, *refs):
    sources, targets = refs[:count], refs[count : 2 * count]
    pick1_ref, pick2_ref, table_ref, semaphores = refs[2 * count :]
    place = lax.axis_index("net")

    @pl.when(place == 0)
    def _():
        pick1_ref[...] = jnp.zeros_like(pick1_ref)
        pick2_ref[...] = jnp.zeros_like(pick2_ref)

    @pl.when(place > 0)
    def _():
        copies = fetch(sources, targets, semaphores)
        halo_ref, theta_ref = targets[:2]
        buses, edges = table_ref.shape
        copies[0].wait()
        ids = column_ids(halo_ref[...], buses)
        rows = lax.broadcasted_iota(jnp.int32, (buses, edges), 0)
        table_ref[...] = jnp.where(rows == ids, 1.0, 0.0).astype(BF16)
        copies[1].wait()
        pick = times(theta_ref[...], table_ref[...])
        pick1_ref[...] = pick[:, : edges // 2]
        pick2_ref[...] = pick[:, edges // 2 :]
        for copy in copies[2:]:
            copy.wait()


def late_kernel(count, *refs):
    sources, here, semaphores = refs[:count], refs[count : 2 * count], refs[-1]
    targets = refs[2 * count + 1 : 3 * count + 1]
    refs[3 * count + 1][...] = refs[2 * count][...]
    place = lax.axis_index("net")

    @pl.when(place == 0)
    def _():
        for copy in fetch(sources, targets, semaphores):
            copy.wait()

    @pl.when(place > 0)
    def _():
        for target, source in zip(targets, here):
            target[...] = source[...]


def tables(refs, theta_ref, halo_ref, from_ref, to_ref):
    (
        edge_ref,
        edge_t_ref,
        own_t_ref,
        inner_ref,
        x_ref,
        p_ref,
        count_edge_ref,
        count_inner_ref,
    ) = refs
    buses = theta_ref.shape[1]
    branches = from_ref.shape[1]
    ids = column_ids(halo_ref[...], buses)
    edges = ids.shape[1]
    lanes = lax.broadcasted_iota(jnp.int32, (edges, buses), 1)
    ids_col = jnp.broadcast_to(ids, (edges, edges)).T[:, :1]
    own = jnp.where(lanes == ids_col, 1.0, 0.0)
    own_t_ref[...] = own.astype(BF16)
    inner = 1.0 - jnp.max(own, axis=0, keepdims=True)
    starts = jnp.where(ids_col == from_ref[...], 1.0, 0.0)
    edge_t_ref[...] = (starts - jnp.where(ids_col == to_ref[...], 1.0, 0.0)).astype(BF16)
    bus_ids = lax.broadcasted_iota(jnp.int32, (1, buses), 1)
    inner_ids = jnp.where(inner > 0.0, bus_ids, -1)
    all_ids = jnp.concatenate([ids, inner_ids], axis=1)
    counts = jnp.zeros((8, all_ids.shape[1]), F32)
    step = 128
    for start in range(0, branches, step):
        part = slice(start, start + step)
        f_col = jnp.broadcast_to(from_ref[:, part], (step, step)).T[:, :1]
        t_col = jnp.broadcast_to(to_ref[:, part], (step, step)).T[:, :1]
        is_f = jnp.where(f_col == all_ids, 1.0, 0.0)
        is_t = jnp.where(t_col == all_ids, 1.0, 0.0)
        signed = (is_f - is_t).astype(BF16)
        edge_ref[part, :] = signed[:, :edges]
        inner_ref[part, :] = signed[:, edges:]
        ends = (is_f + is_t).reshape(step // 8, 8, all_ids.shape[1])
        counts = counts + jnp.sum(ends, axis=0)
    count = jnp.broadcast_to(jnp.sum(counts, axis=0, keepdims=True), counts.shape)
    count_edge_ref[...] = count[:, :edges]
    count_inner_ref[...] = count[:, edges:]
    x = theta_ref[...] * inner
    x_ref[...] = x
    p_ref[...] = times_t(x, inner_ref[...])


def prep_kernel(number, *refs):
    sources, refs = refs[:number], refs[number:]
    theta_ref, halo_ref, from_ref, to_ref, stiff_ref = refs[:5]
    dual_ref, gain_ref, c_ref, rows_ref = refs[5:9]
    outs = refs[9:17]
    targets, semaphores = (*refs[17:-1], dual_ref), refs[-1]
    copies = fetch(sources, targets, semaphores)
    lam_f_ref, lam_t_ref, outage_ref = targets[:3]
    per_bus = targets[3:7]

    @pl.when(lax.axis_index("net") >= 0)
    def _():
        tables(outs, theta_ref, halo_ref, from_ref, to_ref)

    for copy in copies:
        copy.wait()
    p_ref = outs[5]
    weight = stiff_ref[...] * (1.0 - outage_ref[...].astype(F32))
    gain_ref[...] = PENALTY * weight / (PENALTY + 2.0 * weight)
    c_ref[...] = p_ref[...] - (lam_f_ref[...] - lam_t_ref[...]) / PENALTY
    for index, ref in enumerate(per_bus):
        rows_ref[2 * index : 2 * index + 2, :] = jnp.broadcast_to(
            ref[...], (2, rows_ref.shape[1])
        )


def has_far():
    place, places = lax.axis_index("net"), lax.axis_size("net")
    return jnp.where(place % 2 == 0, place > 0, place < places - 1)


def gaps(moved, scale, p_ref, c_ref, gain_ref, flow_ref, deltas):
    for delta_ref in deltas:
        delta_ref[...] = p_ref[...] + moved
    flow = gain_ref[...] * (c_ref[...] + scale * moved)
    flow_ref[...] = flow
    return flow


def gap_step(z, scale, edge_ref, turned_ref, p_ref, c_ref, gain_ref, flow_ref, send_ref, deltas):
    conts, slots = z.shape[0], send_ref.shape[1]

    @pl.when(has_far())
    def _():
        moved = times(z, turned_ref[...])
        flow = gaps(moved, scale, p_ref, c_ref, gain_ref, flow_ref, deltas)
        send_ref[:conts, :] = times(flow, edge_ref[:, slots:])

    @pl.when(jnp.logical_not(has_far()))
    def _():
        send_ref[:conts, :] = jnp.zeros((conts, slots), F32)


def first_kernel(
    far_ref,
    got1_ref,
    pick1_ref,
    edge_ref,
    turned_ref,
    p_ref,
    c_ref,
    gain_ref,
    count_ref,
    send_ref,
    z_ref,
    delta_ref,
    flow_ref,
):
    slots = pick1_ref.shape[1]
    conts = p_ref.shape[0]
    z = jnp.concatenate([pick1_ref[...] + got1_ref[...], far_ref[...]], axis=1)
    z_ref[...] = z
    gap_step(z, 1.0, edge_ref, turned_ref, p_ref, c_ref, gain_ref, flow_ref, send_ref, [delta_ref])
    send_ref[conts:, :] = count_ref[:, slots:]


def both_ends(far_ref, got1_ref, send1_ref, rows):
    return jnp.concatenate(
        [send1_ref[rows, :] + got1_ref[rows, :], far_ref[rows, :]], axis=1
    )


def round_step(
    far_ref, got1_ref, send1_ref, z_ref, degree, edge_ref, turned_ref, p_ref, c_ref, gain_ref, outs
):
    both_ref, z_out_ref, flow_ref, out_ref, *deltas = outs
    both = both_ends(far_ref, got1_ref, send1_ref, slice(0, z_ref.shape[0]))
    both_ref[...] = both
    z = (degree * z_ref[...] - both) / (degree + 1.0)
    z_out_ref[...] = z
    gap_step(z, 2.0, edge_ref, turned_ref, p_ref, c_ref, gain_ref, flow_ref, out_ref, deltas)


def second_kernel(
    far_ref, got1_ref, send1_ref, z_ref, edge_ref, turned_ref, p_ref, c_ref, gain_ref, *outs
):
    *outs, degree_ref = outs
    rows = slice(z_ref.shape[0], send1_ref.shape[0])
    degree = both_ends(far_ref, got1_ref, send1_ref, rows)
    degree_ref[...] = degree
    round_step(
        far_ref,
        got1_ref,
        send1_ref,
        z_ref,
        degree[:1, :],
        edge_ref,
        turned_ref,
        p_ref,
        c_ref,
        gain_ref,
        outs,
    )


def next_kernel(
    far_ref,
    got1_ref,
    send1_ref,
    z_ref,
    degree_ref,
    edge_ref,
    turned_ref,
    p_ref,
    c_ref,
    gain_ref,
    *outs,
):
    round_step(
        far_ref,
        got1_ref,
        send1_ref,
        z_ref,
        degree_ref[:1, :],
        edge_ref,
        turned_ref,
        p_ref,
        c_ref,
        gain_ref,
        outs,
    )


def send_kernel(scale, number, *refs):
    z_ref, edge_ref, turned_ref, p_ref, c_ref, gain_ref = refs[:6]
    held = refs[6 : 6 + number]
    counts = refs[6 + number : -1 - number]
    outs = refs[-1 - number : -1]
    send_ref = refs[-1]
    conts, slots = z_ref.shape[0], send_ref.shape[1]
    table = edge_ref[:, :slots]

    @pl.when(has_far())
    def _():
        send_ref[:conts, :] = times(held[0][...], table)
        for target, source in zip(outs, held):
            target[...] = source[...]

    @pl.when(jnp.logical_not(has_far()))
    def _():
        moved = times(z_ref[:, :slots], turned_ref[:slots, :])
        flow = gaps(moved, scale, p_ref, c_ref, gain_ref, outs[0], outs[1:])
        send_ref[:conts, :] = times(flow, table)

    for ref in counts:
        send_ref[conts:, :] = ref[:, :slots]


def inner_step(flow_ref, x_ref, count_ref, inner_ref):
    net = times(flow_ref[...], inner_ref[...])
    count = count_ref[:1, :]
    return net, (count * x_ref[...] - net) / (count + 1.0)


def beside_kernel(
    flow_ref, delta_ref, x_ref, count_ref, inner_ref, net_ref, x_out_ref, p_ref, c_ref
):
    net, x = inner_step(flow_ref, x_ref, count_ref, inner_ref)
    net_ref[...] = net
    x_out_ref[...] = x
    p = times_t(x, inner_ref[...])
    p_ref[...] = p
    c_ref[...] = 2.0 * (p + flow_ref[...]) - delta_ref[...]


def beside_last_kernel(
    flow_ref,
    x_ref,
    count_ref,
    inner_ref,
    own_ref,
    dual_ref,
    rows_ref,
    *refs,
):
    *refs, net_ref, x_out_ref, dual_out_ref, sums_ref = refs
    rounds = len(refs) // 2
    net, x = inner_step(flow_ref, x_ref, count_ref, inner_ref)
    net_ref[...] = net
    x_out_ref[...] = x
    conts = net.shape[0]
    edge = jnp.concatenate([ref[...] for ref in refs[:rounds]], axis=0)
    spread = times(edge, own_ref[...])
    part = 1.0 / (rows_ref[4:5, :] + PENALTY + BALANCE)
    dual = dual_ref[...]
    wholes = [
        ref[...] + spread[index * conts : (index + 1) * conts]
        for index, ref in enumerate(refs[rounds:])
    ]
    for index, whole in enumerate([*wholes, net]):
        term = 2.0 * part * (BALANCE * whole - dual) + dual
        sums_ref[index : index + 1, :] = jnp.sum(term, axis=0, keepdims=True)
        if index < rounds:
            dual = dual + part * (BALANCE * whole - dual)
    dual_out_ref[...] = dual


def total_kernel(
    far_ref, got1_ref, send1_ref, own_ref, rows_ref, sums_in_ref, both_ref, sums_ref
):
    both = both_ends(far_ref, got1_ref, send1_ref, slice(0, send1_ref.shape[0]))
    both_ref[...] = both
    row = jnp.broadcast_to(jnp.sum(both, axis=0, keepdims=True), (8, both.shape[1]))
    sums_ref[...] = sums_in_ref[...]
    last = slice(ROUNDS - 1, ROUNDS)
    part = 1.0 / (rows_ref[4:5, :] + PENALTY + BALANCE)
    late = times(row, own_ref[...])[:1]
    sums_ref[last, :] = sums_in_ref[last, :] + 2.0 * BALANCE * part * late


def field_kernel(
    both_ref, z_ref, degree_ref, own_ref, x_ref, net_ref, dual_ref, rows_ref, theta_ref, gen_ref
):
    conts = net_ref.shape[0]
    both = both_ref[...]
    degree = degree_ref[:1, :]
    z = (degree * z_ref[...] - both) / (degree + 1.0)
    spread = times(jnp.concatenate([both, z], axis=0), own_ref[...])
    theta_ref[...] = x_ref[...] + spread[conts:]
    part = 1.0 / (rows_ref[4:5, :] + PENALTY + BALANCE)
    gen_ref[...] = part * (BALANCE * (net_ref[...] + spread[:conts]) - dual_ref[...])


def end_kernel(contingencies, *refs):
    *sum_refs, rows_ref, part_gen_ref, gen_ref, base_out_ref = refs
    total = sum_refs[0][...]
    for ref in sum_refs[1:]:
        total = total + ref[...]
    mean = total / contingencies
    base, load = rows_ref[0:1, :], rows_ref[2:3, :]
    limit = rows_ref[6:7, :]
    part = 1.0 / (rows_ref[4:5, :] + PENALTY + BALANCE)
    shared = jnp.zeros_like(base)
    for index in range(ROUNDS):
        gen_shared = part * (PENALTY * base - shared + BALANCE * load)
        if index == ROUNDS - 1:
            gen_ref[...] = part_gen_ref[...] + gen_shared
        total_mean = mean[index : index + 1, :] + 2.0 * gen_shared + shared - base
        shared = shared + PENALTY * (gen_shared - base)
        base = jnp.clip(total_mean, 0.0, limit)
    base_out_ref[...] = base


def call(kernel, outs, *args, scratch=(), spaces=None, flops=2 * 128 * 640 * 512):
    shapes = [jax.ShapeDtypeStruct(shape, dtype) for shape, dtype in outs]
    moved = sum(a.size * a.dtype.itemsize for a in args)
    spaces = spaces or [pltpu.VMEM] * len(args)
    return pl.pallas_call(
        kernel,
        out_shape=shapes,
        in_specs=[pl.BlockSpec(memory_space=space) for space in spaces],
        out_specs=[pl.BlockSpec(memory_space=pltpu.VMEM)] * len(outs),
        scratch_shapes=list(scratch),
        compiler_params=pltpu.CompilerParams(vmem_limit_bytes=32 * 1024 * 1024),
        cost_estimate=pl.CostEstimate(flops=flops, bytes_accessed=moved, transcendentals=0),
    )(*args)


def swaps(conts, nets):
    def pairs(shift):
        found = []
        for c in range(conts):
            for p in range(nets):
                q = p + 1 if p % 2 == shift else p - 1
                if 0 <= q < nets:
                    found.append((c * nets + p, c * nets + q))
                elif (c ^ 1) < conts:
                    found.append((c * nets + p, (c ^ 1) * nets + p))
                else:
                    found.append((c * nets + p, c * nets + p))
        return found

    return pairs(0), pairs(1)


def local(
    angles,
    lam_from,
    lam_to,
    gen_dual,
    base_prev,
    outage,
    from_bus,
    to_ref,
    halo_rows,
    stiffness,
    bus_load,
    gen_cost,
    gen_limit,
):
    conts, buses = angles.shape
    branches = from_bus.shape[0]
    slots = halo_rows.shape[0]
    edges = 2 * slots
    cont_size = lax.axis_size("cont")
    net_size = lax.axis_size("net")
    swap1, swap2 = swaps(cont_size, net_size)
    axes = ("cont", "net")

    def trade_near(value):
        return lax.ppermute(value, axes, swap1)

    def trade_far(value):
        return lax.ppermute(value, axes, swap2)

    def in_hbm(*arrays):
        return [pltpu.with_memory_space_constraint(a, pltpu.HBM) for a in arrays]

    bus = ((conts, buses), F32)
    branch = ((conts, branches), F32)
    half = ((conts, slots), F32)
    edge = ((conts, edges), F32)
    tall = ((conts + 8, slots), F32)
    row = ((8, buses), F32)
    total = ((ROUNDS, buses), F32)

    halo_row = halo_rows.reshape(1, slots)
    fetched = [halo_row, angles, from_bus, to_ref, stiffness]
    count = len(fetched)

    def load(*refs):
        load_kernel(count, *refs)

    def late(*refs):
        late_kernel(count, *refs)

    arrived = [(a.shape, a.dtype) for a in fetched]
    *here, pick1, pick2 = call(
        load,
        arrived + [half, half],
        *in_hbm(*fetched),
        spaces=[pltpu.HBM] * count,
        scratch=[pltpu.VMEM((buses, edges), BF16), pltpu.SemaphoreType.DMA((count,))],
    )
    got2 = trade_far(pick2)
    *here, pick1 = call(
        late,
        arrived + [half],
        *in_hbm(*fetched),
        *here,
        pick1,
        spaces=[pltpu.HBM] * count + [pltpu.VMEM] * (count + 1),
        scratch=[pltpu.SemaphoreType.DMA((count,))],
    )
    got1 = trade_near(pick1)
    halo_row, angles = here[:2]
    from_row, to_row, stiff_row = (a.reshape(1, branches) for a in here[2:])
    rows = [a.reshape(1, buses) for a in (base_prev, bus_load, gen_cost, gen_limit)]
    fetched = [lam_from, lam_to, outage, *rows, gen_dual]
    near_args = [angles, halo_row, from_row, to_row, stiff_row]
    number = len(fetched)

    def prep(*refs):
        prep_kernel(number, *refs)

    (
        gen_dual,
        gain,
        c,
        rows,
        edge_table,
        edge_turned,
        own,
        inner_table,
        x,
        p,
        count_edge,
        count_inner,
    ) = call(
        prep,
        [
            bus,
            branch,
            branch,
            row,
            ((branches, edges), BF16),
            ((edges, branches), BF16),
            ((edges, buses), BF16),
            ((branches, buses), BF16),
            bus,
            branch,
            ((8, edges), F32),
            row,
        ],
        *in_hbm(*fetched),
        *near_args,
        spaces=[pltpu.HBM] * number + [pltpu.VMEM] * len(near_args),
        scratch=[pltpu.VMEM(a.shape, a.dtype) for a in fetched[:-1]]
        + [pltpu.SemaphoreType.DMA((number,))],
    )
    send2, z, delta, flow = call(
        first_kernel,
        [tall, edge, branch, branch],
        pick2 + got2,
        got1,
        pick1,
        edge_table,
        edge_turned,
        p,
        c,
        gain,
        count_edge,
    )
    nets, boths = [], []

    def make_near(first, held, z, p, c, counts):
        def kernel(*refs):
            send_kernel(1.0 if first else 2.0, len(held), *refs)

        args = [z, edge_table, edge_turned, p, c, gain, *held, *counts]
        return call(
            kernel,
            [branch] * len(held) + [tall if first else half],
            *args,
        )

    for index in range(1, ROUNDS):
        first = index == 1
        got2 = trade_far(send2)
        counts = [count_edge] if first else []
        flow, delta, send1 = make_near(first, [flow, delta], z, p, c, counts)
        got1 = trade_near(send1)
        net, x, p, c = call(
            beside_kernel,
            [bus, bus, branch, branch],
            flow,
            delta,
            x,
            count_inner,
            inner_table,
        )
        nets.append(net)
        outs = [edge, edge, branch, half]
        if index < ROUNDS - 1:
            outs = outs + [branch]
        ends = [send2 + got2, got1, send1, z]
        tables = [edge_table, edge_turned, p, c, gain]
        if first:
            both, z, flow, send2, *deltas, degree = call(
                second_kernel, outs + [((8, edges), F32)], *ends, *tables
            )
        else:
            both, z, flow, send2, *deltas = call(next_kernel, outs, *ends, degree, *tables)
        delta = deltas[0] if deltas else None
        boths.append(both)
    got2 = trade_far(send2)
    flow, send1 = make_near(False, [flow], z, p, c, [])
    got1 = trade_near(send1)
    net, x, dual, sums = call(
        beside_last_kernel,
        [bus, bus, bus, total],
        flow,
        x,
        count_inner,
        inner_table,
        own,
        gen_dual,
        rows,
        *boths,
        *nets,
    )
    both, sums = call(
        total_kernel, [edge, total], send2 + got2, got1, send1, own, rows, sums
    )
    parts = [sums]
    for shift in reversed(range(1, cont_size)):
        parts.append(
            lax.ppermute(sums, "cont", [(i, (i + shift) % cont_size) for i in range(cont_size)])
        )

    theta, part_gen = call(
        field_kernel,
        [bus, bus],
        both,
        z,
        degree,
        own,
        x,
        net,
        dual,
        rows,
    )

    def finish(*refs):
        end_kernel(float(conts * cont_size), *refs)

    generation, base = call(finish, [bus, ((1, buses), F32)], *parts, rows, part_gen)
    return theta, generation, base.reshape(buses)


def solution(mesh):
    placed = (
        P("cont", "net"),
        P("cont", "net"),
        P("cont", "net"),
        P("cont", "net"),
        P("net"),
        P("cont", "net"),
        P("net"),
        P("net"),
        P("net"),
        P("net"),
        P("net"),
        P("net"),
        P("net"),
    )
    return jax.shard_map(
        local,
        mesh=mesh,
        in_specs=placed,
        out_specs=(P("cont", "net"), P("cont", "net"), P("net")),
        check_vma=False,
    )
```
